32 devices in a mesh: block: 8 (over y, x, core), dp: 4 (over z).
Axes of the slice: x: 2, y: 2, z: 4, core: 2. Of those that a mesh axis runs over, the one named last changes fastest.
Arguments:
- tokens: bfloat16 [2048, 12288], P('dp', 'block'), may hold values from -6 to 6
- cotangent: bfloat16 [2048, 12288], P('dp', 'block'), may hold values from -12 to 12
- right_one: bfloat16 [96, 128, 384], P('block'), may hold values from -0.5 to 0.5
- left_one: bfloat16 [96, 384, 512], P('block'), may hold values from -0.3125 to 0.3125
- right_two: bfloat16 [96, 512, 384], P('block'), may hold values from -0.25 to 0.25
- left_two: bfloat16 [96, 384, 128], P('block'), may hold values from -0.3125 to 0.3125
- grad_prev: float32 [96, 491520], P('block', 'dp'), may hold values from -12 to 12
- moment_one: float32 [96, 491520], P('block', 'dp'), may hold values from -2 to 2
- moment_two: float32 [96, 491520], P('block', 'dp'), may hold values from 0.05 to 4
Outputs:
- grad_tokens: bfloat16 [2048, 12288], P('dp', 'block')
- grad_right_one: float32 [96, 128, 384], P('block', 'dp')
- grad_left_one: float32 [96, 384, 512], P('block', 'dp')
- grad_right_two: float32 [96, 512, 384], P('block', 'dp')
- grad_left_two: float32 [96, 384, 128], P('block', 'dp')
- new_moment_one: float32 [96, 491520], P('block', 'dp')
- new_moment_two: float32 [96, 491520], P('block', 'dp')
- adam_update: float32 [96, 491520], P('block', 'dp')
The draws below stay inside these ranges and needn't reach their ends.
All inputs are finite; a program needn't handle non-finite values.
Results may differ from the reference program's by a relative error of at most 0.013.
Values may be sent and summed in bfloat16 or wider, within the bound.
No kernel may reach another device: no remote copies, remote signals or barrier semaphores. Data moves between devices by JAX's collectives and lax.ppermute only.
A program may use at most 192 MiB of HBM per device.

```python
import math
import jax
import jax.numpy as jnp

D = 12288
BLOCKS = 96
SPLIT = 4
TOK_DEV = 512
BLOCK_IN = 128
BLOCK_HID = 512
MIDDLE = 384
PER_BLOCK = 491520
TOKENS = 2048
N_DP = 4


def levels(own_key, extent, cuts, smallest, largest):
    level = 1.0
    for dim, shards_of in cuts:
        steps = jax.random.uniform(jax.random.fold_in(jax.random.fold_in(own_key, 6), dim), (shards_of,), jnp.float32, smallest / len(cuts), largest / len(cuts))
        level = level * jnp.repeat(jnp.exp(steps), extent[dim] // shards_of).reshape((-1,) + (1,) * (len(extent) - 1 - dim))
    return level


def normal_values(rng, extent, width, reach, shards=(), held_as=jnp.bfloat16):
    level = levels(rng, extent, shards, -0.22, 0.18) if shards else 1.0
    drawn = jax.random.normal(rng, extent, jnp.float32) * width * level
    return jnp.minimum(jnp.maximum(drawn, -reach), reach).astype(held_as)


def setup_inputs(seed: int = 0) -> dict:
    streams_of = jax.random.split(jax.random.key(seed), 10)
    return {
        "tokens": normal_values(streams_of[0], (TOKENS, D), 1.0, 6.0, ((0, 4), (1, 8))),
        "cotangent": normal_values(streams_of[1], (TOKENS, D), 2.0, 12.0, ((0, 4), (1, 8))),
        "right_one": normal_values(streams_of[2], (BLOCKS, BLOCK_IN, MIDDLE), BLOCK_IN ** -0.5, 0.5, ((0, 8),)),
        "left_one": normal_values(streams_of[3], (BLOCKS, MIDDLE, BLOCK_HID), MIDDLE ** -0.5, 0.3125, ((0, 8),)),
        "right_two": normal_values(streams_of[4], (BLOCKS, BLOCK_HID, MIDDLE), BLOCK_HID ** -0.5, 0.25, ((0, 8),)),
        "left_two": normal_values(streams_of[5], (BLOCKS, MIDDLE, BLOCK_IN), MIDDLE ** -0.5, 0.3125, ((0, 8),)),
        "grad_prev": normal_values(streams_of[6], (BLOCKS, PER_BLOCK), 2.0, 12.0, ((0, 8), (1, 4)), jnp.float32),
        "moment_one": normal_values(streams_of[7], (BLOCKS, PER_BLOCK), 0.3, 2.0, ((0, 8), (1, 4)), jnp.float32),
        "moment_two": jnp.clip(jnp.exp(math.log(4.0) - 4.3820266 * jax.random.uniform(streams_of[8], (BLOCKS, PER_BLOCK), jnp.float32) ** levels(streams_of[8], (BLOCKS, PER_BLOCK), ((0, 8), (1, 4)), -0.2, 0.2)), 0.05, 4.0),
    }


def gelu_tanh(values):
    return jax.nn.gelu(values, approximate=True)

def group_pass(inputs, grad_out, right_one, left_one, right_two, left_two, loss_scale):
    rows = inputs.shape[0]
    f32 = jnp.float32
    bf16 = jnp.bfloat16
    token_blocks = inputs.reshape(rows, BLOCKS, BLOCK_IN).astype(f32)
    right_first = right_one.astype(f32)
    left_first = left_one.reshape(BLOCKS, BLOCKS, SPLIT, BLOCK_HID).astype(f32)
    right_second = right_two.astype(f32)
    left_second = left_two.reshape(BLOCKS, BLOCKS, SPLIT, BLOCK_IN).astype(f32)
    first_mid = jnp.einsum('tbk,bkj->tbj', token_blocks, right_first).astype(bf16)
    first_view = first_mid.reshape(rows, BLOCKS, BLOCKS, SPLIT).astype(f32)
    hidden_pre = jnp.einsum('tbcq,cbqf->tcf', first_view, left_first)
    hidden = gelu_tanh(hidden_pre).astype(bf16).astype(f32)
    second_mid = jnp.einsum('tcf,cfj->tcj', hidden, right_second).astype(bf16)
    second_view = second_mid.reshape(rows, BLOCKS, BLOCKS, SPLIT).astype(f32)
    grad_blocks = grad_out.reshape(rows, BLOCKS, BLOCK_IN).astype(f32)
    grad_second = jnp.einsum('tdk,dcqk->tcdq', grad_blocks, left_second).astype(bf16)
    grad_second = grad_second.reshape(rows, BLOCKS, MIDDLE).astype(f32)
    part_left_two = jnp.einsum('tcdq,tdk->dcqk', second_view, grad_blocks) * loss_scale
    part_right_two = jnp.einsum('tcf,tcj->cfj', hidden, grad_second) * loss_scale
    grad_hidden = jnp.einsum('tcj,cfj->tcf', grad_second, right_second)
    unused_value, back_gelu = jax.vjp(gelu_tanh, hidden_pre)
    grad_pre = back_gelu(grad_hidden)[0].astype(bf16).astype(f32)
    part_left_one = jnp.einsum('tbcq,tcf->cbqf', first_view, grad_pre) * loss_scale
    grad_first = jnp.einsum('tcf,cbqf->tbcq', grad_pre, left_first).astype(bf16)
    grad_first = grad_first.reshape(rows, BLOCKS, MIDDLE).astype(f32)
    part_right_one = jnp.einsum('tbk,tbj->bkj', token_blocks, grad_first) * loss_scale
    grad_inputs = jnp.einsum('tbj,bkj->tbk', grad_first, right_first).astype(bf16)
    partials = (part_right_one, part_left_one.reshape(BLOCKS, MIDDLE, BLOCK_HID), part_right_two, part_left_two.reshape(BLOCKS, MIDDLE, BLOCK_IN))
    return (grad_inputs.reshape(rows, D), partials)

def reference(tokens, cotangent, right_one, left_one, right_two, left_two, grad_prev, moment_one, moment_two):
    loss_scale = float(TOKENS) ** (-0.5)
    grad_pieces = []
    totals = None
    for group_index in range(N_DP):
        start = group_index * TOK_DEV
        grad_inputs, partials = group_pass(tokens[start:start + TOK_DEV], cotangent[start:start + TOK_DEV], right_one, left_one, right_two, left_two, loss_scale)
        grad_pieces.append(grad_inputs)
        rounded = tuple((piece.astype(jnp.bfloat16).astype(jnp.float32) for piece in partials))
        if totals is None:
            totals = rounded
        else:
            totals = tuple((older + newer for older, newer in zip(totals, rounded)))
    grad_tokens = jnp.concatenate(grad_pieces, axis=0)
    new_moment_one = 0.9 * moment_one + 0.1 * grad_prev
    new_moment_two = 0.95 * moment_two + 0.05 * grad_prev * grad_prev
    first_hat = new_moment_one / (1.0 - 0.9 ** 10)
    second_hat = new_moment_two / (1.0 - 0.95 ** 10)
    adam_update = first_hat / (jnp.sqrt(second_hat) + 1e-08)
    return (grad_tokens, totals[0], totals[1], totals[2], totals[3], new_moment_one, new_moment_two, adam_update)
```

```python
import functools
import math

import jax
import jax.numpy as jnp
from jax import lax
from jax.experimental import pallas as pl
from jax.experimental.pallas import tpu as pltpu
from jax.sharding import PartitionSpec as P

BLOCKS = 96
SPLIT = 4
BLOCK_IN = 128
BLOCK_HID = 512
MIDDLE = 384

F32 = jnp.float32
BF16 = jnp.bfloat16
GROUP = 4
LANES = 128
VMEM_LIMIT = 48 * 1024 * 1024
CHUNKS = (2, 4, 6)


def dot(lhs, rhs, lhs_dim, rhs_dim):
    return lax.dot_general(
        lhs, rhs, (((lhs_dim,), (rhs_dim,)), ((), ())), preferred_element_type=F32
    )


def permutation(outer, inner):
    size = outer * inner * SPLIT
    row = lax.broadcasted_iota(jnp.int32, (size, size), 0)
    col = lax.broadcasted_iota(jnp.int32, (size, size), 1)
    at_outer = row // (inner * SPLIT)
    at_inner = (row // SPLIT) % inner
    source = at_inner * (outer * SPLIT) + at_outer * SPLIT + row % SPLIT
    return jnp.where(col == source, 1.0, 0.0).astype(BF16)


def first_kernel(chunks, ways, me_ref, x_ref, g_ref, right_ref, left_ref, *refs):
    outs, (rows,) = refs[:-1], refs[-1:]
    here = sum(chunks)
    span = here * SPLIT
    perm = permutation(here, GROUP)
    for which in range(2):
        for b in range(GROUP):
            lanes = slice(b * BLOCK_IN, (b + 1) * BLOCK_IN)
            if which == 0:
                value = dot(right_ref[b], x_ref[:, lanes], 0, 1)
            else:
                value = dot(left_ref[b], g_ref[:, lanes], 1, 1)
            rows[which, b] = value.astype(BF16)
        for m in range(ways):
            start = pl.multiple_of((me_ref[0] ^ m) * span, 16)
            taken = jnp.concatenate(
                [rows[which, b, pl.ds(start, span), :] for b in range(GROUP)], axis=0
            )
            mixed = dot(perm, taken, 1, 0).astype(BF16)
            at = 0
            for k, size in enumerate(chunks):
                part = mixed[at * GROUP * SPLIT : (at + size) * GROUP * SPLIT]
                outs[k * ways + m][which] = part.reshape(size, GROUP * SPLIT, part.shape[-1])
                at += size


def middle_kernel(ways, n_dp, scale, me_ref, *refs):
    takes = refs[:ways]
    left_ref, right_ref = refs[ways : ways + 2]
    gives = refs[ways + 2 : 2 * ways + 2]
    grads_ref = refs[2 * ways + 2]
    first_in, grad_in, second_out, grad_out = refs[2 * ways + 3 :]
    span = MIDDLE // ways
    for m in range(ways):
        start = pl.multiple_of((me_ref[0] ^ m) * span, 16)
        first_in[pl.ds(start, span), :] = takes[m][0, 0]
        grad_in[pl.ds(start, span), :] = takes[m][1, 0]
    left = left_ref[0]
    right = right_ref[0]
    pre = dot(left, first_in[...], 0, 0)
    root = math.sqrt(2.0 / math.pi)
    square = pre * pre
    bend = jnp.tanh(root * (pre + 0.044715 * (square * pre)))
    half = 0.5 * (1.0 + bend)
    hidden = (pre * half).astype(BF16)
    slope = half + 0.5 * pre * (1.0 - bend * bend) * (root * (1.0 + 3 * 0.044715 * square))
    second_out[...] = dot(right, hidden, 0, 0).astype(BF16)
    grad_second = grad_in[...]
    grad_pre = (dot(right, grad_second, 1, 0) * slope).astype(BF16)
    grad_out[...] = dot(left, grad_pre, 1, 0).astype(BF16)
    for m in range(ways):
        start = pl.multiple_of((me_ref[0] ^ m) * span, 16)
        gives[m][0, 0] = second_out[pl.ds(start, span), :]
        gives[m][1, 0] = grad_out[pl.ds(start, span), :]
    grad_right = (dot(hidden, grad_second, 1, 1) * scale).astype(BF16)
    grad_left = (dot(first_in[...], grad_pre, 1, 1) * scale).astype(BF16)
    at = 0
    for grad in (grad_right, grad_left):
        depth = grad.shape[0] // n_dp
        for lane in range(0, grad.shape[1], LANES):
            for z in range(n_dp):
                grads_ref[z, 0, at : at + depth, :] = grad[
                    z * depth : (z + 1) * depth, lane : lane + LANES
                ]
            at += depth


def last_kernel(chunks, ways, n_dp, scale, me_ref, x_ref, g_ref, right_ref, *refs):
    count = len(chunks) * ways
    takes = refs[:count]
    tokens_ref, grads_ref, rows = refs[count:]
    here = sum(chunks)
    span = here * SPLIT
    perm = permutation(GROUP, here)
    for which in range(2):
        for m in range(ways):
            start = pl.multiple_of((me_ref[0] ^ m) * span, 16)
            taken = jnp.concatenate(
                [
                    takes[k * ways + m][which].reshape(size * GROUP * SPLIT, -1)
                    for k, size in enumerate(chunks)
                ],
                axis=0,
            )
            mixed = dot(perm, taken, 1, 0).astype(BF16)
            for b in range(GROUP):
                rows[which, b, pl.ds(start, span), :] = mixed[b * span : (b + 1) * span]
    for b in range(GROUP):
        lanes = slice(b * BLOCK_IN, (b + 1) * BLOCK_IN)
        second_in = rows[0, b]
        grad_first = rows[1, b]
        tokens_ref[:, lanes] = dot(grad_first, right_ref[b], 0, 1).astype(BF16)
        grad_left = (dot(second_in, g_ref[:, lanes], 1, 0) * scale).astype(BF16)
        grad_right = (dot(x_ref[:, lanes], grad_first, 0, 1) * scale).astype(BF16)
        at = 0
        for grad in (grad_left, grad_right):
            depth = grad.shape[0] // n_dp
            for lane in range(0, grad.shape[1], LANES):
                for z in range(n_dp):
                    grads_ref[z, b, at : at + depth, :] = grad[
                        z * depth : (z + 1) * depth, lane : lane + LANES
                    ]
                at += depth


def widen_kernel(n_old, sum_ref, *refs):
    at = 0
    for out_ref in refs[n_old:]:
        depth, width = out_ref.shape[1:]
        for lane in range(0, width, LANES):
            out_ref[:, :, lane : lane + LANES] = sum_ref[0, :, at : at + depth, :].astype(F32)
            at += depth


def params():
    return pltpu.CompilerParams(vmem_limit_bytes=VMEM_LIMIT)


def cost(flops, moved, transcendentals=0):
    return pl.CostEstimate(
        flops=int(flops), bytes_accessed=int(moved), transcendentals=int(transcendentals)
    )


def widen(summed, shapes, here, first_block, old, per_step):
    size, depth, _ = summed.shape[1:]
    n_old = len(old)
    any_spec = pl.BlockSpec(memory_space=pl.ANY)
    at = first_block // per_step
    return pl.pallas_call(
        functools.partial(widen_kernel, n_old),
        grid=(size // per_step,),
        in_specs=[pl.BlockSpec((1, per_step, depth, LANES), lambda i: (0, i, 0, 0))]
        + [any_spec] * n_old,
        out_specs=[
            pl.BlockSpec((per_step,) + tuple(shape), lambda i, at=at: (i + at, 0, 0))
            for shape in shapes
        ],
        out_shape=[jax.ShapeDtypeStruct((here,) + tuple(shape), F32) for shape in shapes],
        input_output_aliases={i + 1: i for i in range(n_old)},
        compiler_params=params(),
        cost_estimate=cost(0, summed.size * 6),
        name="widen",
    )(summed, *old)


def on_device_fast(
    tokens, cotangent, right_one, left_one, right_two, left_two, grad_prev, moment_one, moment_two
):
    rows = tokens.shape[0]
    here = right_one.shape[0]
    ways = lax.axis_size("block")
    n_dp = lax.axis_size("dp")
    span = here * SPLIT
    scale = float(n_dp * rows) ** (-0.5)
    me = lax.axis_index("block").astype(jnp.int32).reshape(1)
    unit = here // sum(CHUNKS)
    chunks = tuple(size * unit for size in CHUNKS)
    n_groups = here // GROUP
    tile = GROUP * SPLIT
    wide = GROUP * BLOCK_IN

    new_moment_one = 0.9 * moment_one + 0.1 * grad_prev
    new_moment_two = 0.95 * moment_two + 0.05 * grad_prev * grad_prev
    first_hat = new_moment_one / (1.0 - 0.9**10)
    second_hat = new_moment_two / (1.0 - 0.95**10)
    adam_update = first_hat / (jnp.sqrt(second_hat) + 1e-08)

    token_spec = pl.BlockSpec((rows, wide), lambda i, me: (0, i))
    right_spec = pl.BlockSpec((GROUP, BLOCK_IN, MIDDLE), lambda i, me: (i, 0, 0))
    left_spec = pl.BlockSpec((GROUP, MIDDLE, BLOCK_IN), lambda i, me: (i, 0, 0))
    part_specs = [
        pl.BlockSpec((2, size, tile, rows), lambda i, me: (0, 0, i, 0))
        for size in chunks
        for _ in range(ways)
    ]
    part_shapes = [
        jax.ShapeDtypeStruct((2, size, span, rows), BF16) for size in chunks for _ in range(ways)
    ]
    moved = 2 * here * MIDDLE * rows
    sends = pl.pallas_call(
        functools.partial(first_kernel, chunks, ways),
        grid_spec=pltpu.PrefetchScalarGridSpec(
            num_scalar_prefetch=1,
            grid=(n_groups,),
            in_specs=[token_spec, token_spec, right_spec, left_spec],
            out_specs=part_specs,
            scratch_shapes=[pltpu.VMEM((2, GROUP, MIDDLE, rows), BF16)],
        ),
        out_shape=part_shapes,
        compiler_params=params(),
        cost_estimate=cost(moved * BLOCK_IN * 5, 2 * moved),
        name="first",
    )(me, tokens, cotangent, right_one, left_two)

    last_sent = [None] * ways

    def exchange(parts):
        got = [parts[0]]
        for m in range(1, ways):
            part = parts[m]
            if last_sent[m] is not None:
                part, _ = lax.optimization_barrier((part, last_sent[m]))
            taken = lax.ppermute(part, "block", [(i, i ^ m) for i in range(ways)])
            last_sent[m] = taken
            got.append(taken)
        return got

    offsets = [sum(chunks[:k]) for k in range(len(chunks))]
    arrived = [exchange(sends[k * ways : (k + 1) * ways]) for k in range(len(chunks))]

    share = (BLOCK_HID * MIDDLE + MIDDLE * BLOCK_HID) // n_dp // LANES
    middles = []
    for k, size in enumerate(chunks):
        at = offsets[k]
        slice_spec = pl.BlockSpec((2, 1, span, rows), lambda i, me: (0, i, 0, 0))
        flops = 12 * size * MIDDLE * BLOCK_HID * rows
        outs = pl.pallas_call(
            functools.partial(middle_kernel, ways, n_dp, scale),
            grid_spec=pltpu.PrefetchScalarGridSpec(
                num_scalar_prefetch=1,
                grid=(size,),
                in_specs=[slice_spec] * ways
                + [
                    pl.BlockSpec((1, MIDDLE, BLOCK_HID), lambda i, me, at=at: (i + at, 0, 0)),
                    pl.BlockSpec((1, BLOCK_HID, MIDDLE), lambda i, me, at=at: (i + at, 0, 0)),
                ],
                out_specs=[slice_spec] * ways
                + [pl.BlockSpec((n_dp, 1, share, LANES), lambda i, me: (0, i, 0, 0))],
                scratch_shapes=[pltpu.VMEM((MIDDLE, rows), BF16)] * 4,
            ),
            out_shape=[jax.ShapeDtypeStruct((2, size, span, rows), BF16)] * ways
            + [jax.ShapeDtypeStruct((n_dp, size, share, LANES), BF16)],
            compiler_params=params(),
            cost_estimate=cost(flops, size * MIDDLE * (8 * rows + 8 * BLOCK_HID)),
            name="middle",
        )(me, *arrived[k], left_one, right_two)
        middles.append(outs)

    def summed(grads):
        return lax.psum_scatter(grads, "dp", scatter_dimension=0, tiled=True)

    returned = [exchange(outs[:ways]) for outs in middles]
    big_sums = [summed(outs[ways]) for outs in middles]

    small_share = 2 * MIDDLE * BLOCK_IN // n_dp // LANES
    grad_tokens, small_grads = pl.pallas_call(
        functools.partial(last_kernel, chunks, ways, n_dp, scale),
        grid_spec=pltpu.PrefetchScalarGridSpec(
            num_scalar_prefetch=1,
            grid=(n_groups,),
            in_specs=[token_spec, token_spec, right_spec] + part_specs,
            out_specs=[
                token_spec,
                pl.BlockSpec((n_dp, GROUP, small_share, LANES), lambda i, me: (0, i, 0, 0)),
            ],
            scratch_shapes=[pltpu.VMEM((2, GROUP, MIDDLE, rows), BF16)],
        ),
        out_shape=[
            jax.ShapeDtypeStruct(tokens.shape, BF16),
            jax.ShapeDtypeStruct((n_dp, here, small_share, LANES), BF16),
        ],
        compiler_params=params(),
        cost_estimate=cost(moved * BLOCK_IN * 6, 2 * moved),
        name="last",
    )(me, tokens, cotangent, right_one, *[part for parts in returned for part in parts])
    small_sum = summed(small_grads)

    big_shapes = ((BLOCK_HID // n_dp, MIDDLE), (MIDDLE // n_dp, BLOCK_HID))
    big = ()
    for k, size in enumerate(chunks):
        big = widen(big_sums[k], big_shapes, here, offsets[k], big, 1)
    grad_right_two, grad_left_one = big
    small_shapes = ((MIDDLE // n_dp, BLOCK_IN), (BLOCK_IN // n_dp, MIDDLE))
    grad_left_two, grad_right_one = widen(small_sum, small_shapes, here, 0, (), GROUP)
    return (
        grad_tokens,
        grad_right_one,
        grad_left_one,
        grad_right_two,
        grad_left_two,
        new_moment_one,
        new_moment_two,
        adam_update,
    )


def gelu_tanh(values):
    return jax.nn.gelu(values, approximate=True)


def on_device_plain(
    tokens, cotangent, right_one, left_one, right_two, left_two, grad_prev, moment_one, moment_two
):
    f32 = jnp.float32
    bf16 = jnp.bfloat16
    row_count = tokens.shape[0]
    blocks_here = right_one.shape[0]
    loss_scale = float(lax.axis_size("dp") * row_count) ** (-0.5)
    new_moment_one = 0.9 * moment_one + 0.1 * grad_prev
    new_moment_two = 0.95 * moment_two + 0.05 * grad_prev * grad_prev
    first_hat = new_moment_one / (1.0 - 0.9**10)
    second_hat = new_moment_two / (1.0 - 0.95**10)
    adam_update = first_hat / (jnp.sqrt(second_hat) + 1e-08)
    token_blocks = tokens.reshape(row_count, blocks_here, BLOCK_IN)
    first_mid = jnp.einsum(
        "tbk,bkj->bjt", token_blocks, right_one, preferred_element_type=f32
    ).astype(bf16)
    first_in = lax.all_to_all(
        first_mid.reshape(blocks_here, BLOCKS, SPLIT, row_count),
        "block",
        split_axis=1,
        concat_axis=0,
        tiled=True,
    )
    left_first = left_one.reshape(blocks_here, BLOCKS, SPLIT, BLOCK_HID)
    hidden_pre = jnp.einsum("bcqt,cbqf->cft", first_in, left_first, preferred_element_type=f32)
    hidden = gelu_tanh(hidden_pre).astype(bf16)
    second_mid = jnp.einsum("cft,cfj->cjt", hidden, right_two, preferred_element_type=f32).astype(
        bf16
    )
    second_in = lax.all_to_all(
        second_mid.reshape(blocks_here, BLOCKS, SPLIT, row_count),
        "block",
        split_axis=1,
        concat_axis=0,
        tiled=True,
    )
    left_second = left_two.reshape(blocks_here, BLOCKS, SPLIT, BLOCK_IN)
    grad_blocks = cotangent.reshape(row_count, blocks_here, BLOCK_IN)
    grad_second_out = jnp.einsum(
        "tdk,dcqk->cdqt", grad_blocks, left_second, preferred_element_type=f32
    ).astype(bf16)
    grad_left_two = (
        jnp.einsum("cdqt,tdk->dcqk", second_in, grad_blocks, preferred_element_type=f32)
        * loss_scale
    )
    grad_left_two = grad_left_two.reshape(blocks_here, MIDDLE, BLOCK_IN)
    grad_second = lax.all_to_all(grad_second_out, "block", split_axis=0, concat_axis=1, tiled=True)
    grad_second = grad_second.reshape(blocks_here, MIDDLE, row_count)
    grad_right_two = (
        jnp.einsum("cft,cjt->cfj", hidden, grad_second, preferred_element_type=f32) * loss_scale
    )
    grad_hidden = jnp.einsum("cjt,cfj->cft", grad_second, right_two, preferred_element_type=f32)
    unused_value, back_gelu = jax.vjp(gelu_tanh, hidden_pre)
    grad_pre = back_gelu(grad_hidden)[0].astype(bf16)
    grad_left_one = (
        jnp.einsum("bcqt,cft->cbqf", first_in, grad_pre, preferred_element_type=f32) * loss_scale
    )
    grad_left_one = grad_left_one.reshape(blocks_here, MIDDLE, BLOCK_HID)
    grad_first_out = jnp.einsum(
        "cft,cbqf->bcqt", grad_pre, left_first, preferred_element_type=f32
    ).astype(bf16)
    grad_first = lax.all_to_all(grad_first_out, "block", split_axis=0, concat_axis=1, tiled=True)
    grad_first = grad_first.reshape(blocks_here, MIDDLE, row_count)
    grad_right_one = (
        jnp.einsum("tbk,bjt->bkj", token_blocks, grad_first, preferred_element_type=f32)
        * loss_scale
    )
    grad_inputs = jnp.einsum(
        "bjt,bkj->tbk", grad_first, right_one, preferred_element_type=f32
    ).astype(bf16)
    grad_tokens = grad_inputs.reshape(row_count, blocks_here * BLOCK_IN)
    sum_right_one, sum_left_one, sum_right_two, sum_left_two = (
        lax.psum_scatter(
            grad_right_one.astype(jnp.bfloat16), "dp", scatter_dimension=1, tiled=True
        ).astype(jnp.float32),
        lax.psum_scatter(
            grad_left_one.astype(jnp.bfloat16), "dp", scatter_dimension=1, tiled=True
        ).astype(jnp.float32),
        lax.psum_scatter(
            grad_right_two.astype(jnp.bfloat16), "dp", scatter_dimension=1, tiled=True
        ).astype(jnp.float32),
        lax.psum_scatter(
            grad_left_two.astype(jnp.bfloat16), "dp", scatter_dimension=1, tiled=True
        ).astype(jnp.float32),
    )
    return (
        grad_tokens,
        sum_right_one,
        sum_left_one,
        sum_right_two,
        sum_left_two,
        new_moment_one,
        new_moment_two,
        adam_update,
    )


def solution(mesh):
    in_specs = (
        P("dp", "block"),
        P("dp", "block"),
        P("block", None, None),
        P("block", None, None),
        P("block", None, None),
        P("block", None, None),
        P("block", "dp"),
        P("block", "dp"),
        P("block", "dp"),
    )
    out_specs = (
        P("dp", "block"),
        P("block", "dp", None),
        P("block", "dp", None),
        P("block", "dp", None),
        P("block", "dp", None),
        P("block", "dp"),
        P("block", "dp"),
        P("block", "dp"),
    )
    here = BLOCKS // mesh.shape["block"]
    ways = mesh.shape["block"]
    fits = here % sum(CHUNKS) == 0 and here % GROUP == 0 and ways & (ways - 1) == 0
    return jax.shard_map(
        on_device_fast if fits else on_device_plain, mesh=mesh, in_specs=in_specs, out_specs=out_specs, check_vma=False
    )
```

```python
import functools
import math

import jax
import jax.numpy as jnp
from jax import lax
from jax.experimental import pallas as pl
from jax.experimental.pallas import tpu as pltpu
from jax.sharding import PartitionSpec as P

BLOCKS = 96
SPLIT = 4
BLOCK_IN = 128
BLOCK_HID = 512
MIDDLE = 384

F32 = jnp.float32
BF16 = jnp.bfloat16
GROUP = 4
LANES = 128
VMEM_LIMIT = 62 * 1024 * 1024
CHUNKS = (2, 4, 6)


def dot(lhs, rhs, lhs_dim, rhs_dim):
    return lax.dot_general(
        lhs, rhs, (((lhs_dim,), (rhs_dim,)), ((), ())), preferred_element_type=F32
    )


def permutation(outer, inner):
    size = outer * inner * SPLIT
    row = lax.broadcasted_iota(jnp.int32, (size, size), 0)
    col = lax.broadcasted_iota(jnp.int32, (size, size), 1)
    at_outer = row // (inner * SPLIT)
    at_inner = (row // SPLIT) % inner
    source = at_inner * (outer * SPLIT) + at_outer * SPLIT + row % SPLIT
    return jnp.where(col == source, 1.0, 0.0).astype(BF16)


def first_kernel(chunks, ways, me_ref, x_ref, g_ref, right_ref, left_ref, *refs):
    outs, (rows,) = refs[:-1], refs[-1:]
    here = sum(chunks)
    span = here * SPLIT
    perm = permutation(here, GROUP)
    for which in range(2):
        for b in range(GROUP):
            lanes = slice(b * BLOCK_IN, (b + 1) * BLOCK_IN)
            if which == 0:
                value = dot(right_ref[b], x_ref[:, lanes], 0, 1)
            else:
                value = dot(left_ref[b], g_ref[:, lanes], 1, 1)
            rows[which, b] = value.astype(BF16)
        for m in range(ways):
            start = pl.multiple_of((me_ref[0] ^ m) * span, 16)
            taken = jnp.concatenate(
                [rows[which, b, pl.ds(start, span), :] for b in range(GROUP)], axis=0
            )
            mixed = dot(perm, taken, 1, 0).astype(BF16)
            at = 0
            for k, size in enumerate(chunks):
                part = mixed[at * GROUP * SPLIT : (at + size) * GROUP * SPLIT]
                outs[k * ways + m][which] = part.reshape(size, GROUP * SPLIT, part.shape[-1])
                at += size


def middle_kernel(ways, n_dp, scale, me_ref, *refs):
    takes = refs[:ways]
    left_ref, right_ref = refs[ways : ways + 2]
    gives = refs[ways + 2 : 2 * ways + 2]
    grads_ref = refs[2 * ways + 2]
    first_in, grad_in, second_out, grad_out = refs[2 * ways + 3 :]
    span = MIDDLE // ways
    for m in range(ways):
        start = pl.multiple_of((me_ref[0] ^ m) * span, 16)
        first_in[pl.ds(start, span), :] = takes[m][0, 0]
        grad_in[pl.ds(start, span), :] = takes[m][1, 0]
    left = left_ref[0]
    right = right_ref[0]
    pre = dot(left, first_in[...], 0, 0)
    root = math.sqrt(2.0 / math.pi)
    square = pre * pre
    bend = jnp.tanh(root * (pre + 0.044715 * (square * pre)))
    half = 0.5 * (1.0 + bend)
    hidden = (pre * half).astype(BF16)
    slope = half + 0.5 * pre * (1.0 - bend * bend) * (root * (1.0 + 3 * 0.044715 * square))
    second_out[...] = dot(right, hidden, 0, 0).astype(BF16)
    grad_second = grad_in[...]
    grad_pre = (dot(right, grad_second, 1, 0) * slope).astype(BF16)
    grad_out[...] = dot(left, grad_pre, 1, 0).astype(BF16)
    for m in range(ways):
        start = pl.multiple_of((me_ref[0] ^ m) * span, 16)
        gives[m][0, 0] = second_out[pl.ds(start, span), :]
        gives[m][1, 0] = grad_out[pl.ds(start, span), :]
    grad_right = (dot(hidden, grad_second, 1, 1) * scale).astype(BF16)
    grad_left = (dot(first_in[...], grad_pre, 1, 1) * scale).astype(BF16)
    at = 0
    for grad in (grad_right, grad_left):
        depth = grad.shape[0] // n_dp
        for lane in range(0, grad.shape[1], LANES):
            for z in range(n_dp):
                grads_ref[z, 0, at : at + depth, :] = grad[
                    z * depth : (z + 1) * depth, lane : lane + LANES
                ]
            at += depth


def last_kernel(chunks, ways, n_dp, scale, me_ref, x_ref, g_ref, right_ref, *refs):
    count = len(chunks) * ways
    takes = refs[:count]
    tokens_ref, grads_ref, rows = refs[count:]
    here = sum(chunks)
    span = here * SPLIT
    perm = permutation(GROUP, here)
    for which in range(2):
        for m in range(ways):
            start = pl.multiple_of((me_ref[0] ^ m) * span, 16)
            taken = jnp.concatenate(
                [
                    takes[k * ways + m][which].reshape(size * GROUP * SPLIT, -1)
                    for k, size in enumerate(chunks)
                ],
                axis=0,
            )
            mixed = dot(perm, taken, 1, 0).astype(BF16)
            for b in range(GROUP):
                rows[which, b, pl.ds(start, span), :] = mixed[b * span : (b + 1) * span]
    for b in range(GROUP):
        lanes = slice(b * BLOCK_IN, (b + 1) * BLOCK_IN)
        second_in = rows[0, b]
        grad_first = rows[1, b]
        tokens_ref[:, lanes] = dot(grad_first, right_ref[b], 0, 1).astype(BF16)
        grad_left = (dot(second_in, g_ref[:, lanes], 1, 0) * scale).astype(BF16)
        grad_right = (dot(x_ref[:, lanes], grad_first, 0, 1) * scale).astype(BF16)
        at = 0
        for grad in (grad_left, grad_right):
            depth = grad.shape[0] // n_dp
            for lane in range(0, grad.shape[1], LANES):
                for z in range(n_dp):
                    grads_ref[z, b, at : at + depth, :] = grad[
                        z * depth : (z + 1) * depth, lane : lane + LANES
                    ]
                at += depth


def widen_kernel(n_old, sum_ref, *refs):
    at = 0
    for out_ref in refs[n_old:]:
        depth, width = out_ref.shape[1:]
        for lane in range(0, width, LANES):
            out_ref[:, :, lane : lane + LANES] = sum_ref[0, :, at : at + depth, :].astype(F32)
            at += depth


def in_hbm(arrays):
    return [pltpu.with_memory_space_constraint(array, pltpu.HBM) for array in arrays]


def params():
    return pltpu.CompilerParams(vmem_limit_bytes=VMEM_LIMIT)


def cost(flops, moved, transcendentals=0):
    return pl.CostEstimate(
        flops=int(flops), bytes_accessed=int(moved), transcendentals=int(transcendentals)
    )


def widen(summed, shapes, here, first_block, old, per_step):
    size, depth, _ = summed.shape[1:]
    n_old = len(old)
    any_spec = pl.BlockSpec(memory_space=pl.ANY)
    at = first_block // per_step
    return pl.pallas_call(
        functools.partial(widen_kernel, n_old),
        grid=(size // per_step,),
        in_specs=[pl.BlockSpec((1, per_step, depth, LANES), lambda i: (0, i, 0, 0))]
        + [any_spec] * n_old,
        out_specs=[
            pl.BlockSpec((per_step,) + tuple(shape), lambda i, at=at: (i + at, 0, 0))
            for shape in shapes
        ],
        out_shape=[jax.ShapeDtypeStruct((here,) + tuple(shape), F32) for shape in shapes],
        input_output_aliases={i + 1: i for i in range(n_old)},
        compiler_params=params(),
        cost_estimate=cost(0, summed.size * 6),
        name="widen",
    )(summed, *old)


def on_device_fast(
    tokens, cotangent, right_one, left_one, right_two, left_two, grad_prev, moment_one, moment_two
):
    rows = tokens.shape[0]
    here = right_one.shape[0]
    ways = lax.axis_size("block")
    n_dp = lax.axis_size("dp")
    span = here * SPLIT
    scale = float(n_dp * rows) ** (-0.5)
    me = lax.axis_index("block").astype(jnp.int32).reshape(1)
    unit = here // sum(CHUNKS)
    chunks = tuple(size * unit for size in CHUNKS)
    n_groups = here // GROUP
    tile = GROUP * SPLIT
    wide = GROUP * BLOCK_IN

    new_moment_one = 0.9 * moment_one + 0.1 * grad_prev
    new_moment_two = 0.95 * moment_two + 0.05 * grad_prev * grad_prev
    first_hat = new_moment_one / (1.0 - 0.9**10)
    second_hat = new_moment_two / (1.0 - 0.95**10)
    adam_update = first_hat / (jnp.sqrt(second_hat) + 1e-08)

    token_spec = pl.BlockSpec((rows, wide), lambda i, me: (0, i))
    right_spec = pl.BlockSpec((GROUP, BLOCK_IN, MIDDLE), lambda i, me: (i, 0, 0))
    left_spec = pl.BlockSpec((GROUP, MIDDLE, BLOCK_IN), lambda i, me: (i, 0, 0))
    part_specs = [
        pl.BlockSpec((2, size, tile, rows), lambda i, me: (0, 0, i, 0))
        for size in chunks
        for _ in range(ways)
    ]
    part_shapes = [
        pltpu.HBM((2, size, span, rows), BF16) for size in chunks for _ in range(ways)
    ]
    moved = 2 * here * MIDDLE * rows
    sends = pl.pallas_call(
        functools.partial(first_kernel, chunks, ways),
        grid_spec=pltpu.PrefetchScalarGridSpec(
            num_scalar_prefetch=1,
            grid=(n_groups,),
            in_specs=[token_spec, token_spec, right_spec, left_spec],
            out_specs=part_specs,
            scratch_shapes=[pltpu.VMEM((2, GROUP, MIDDLE, rows), BF16)],
        ),
        out_shape=part_shapes,
        compiler_params=params(),
        cost_estimate=cost(moved * BLOCK_IN * 5, 2 * moved),
        name="first",
    )(me, tokens, cotangent, right_one, left_two)

    def permute(parts, ms):
        return {m: lax.ppermute(parts[m], "block", [(i, i ^ m) for i in range(ways)]) for m in ms}

    def after(arrays, *done):
        held = lax.optimization_barrier((arrays, done))
        return held[0]

    early = [m for m in range(1, ways) if m & (m - 1) == 0 and m > 1]
    late = [m for m in range(1, ways) if m not in early]
    offsets = [sum(chunks[:k]) for k in range(len(chunks))]
    n_parts = len(chunks)

    share = (BLOCK_HID * MIDDLE + MIDDLE * BLOCK_HID) // n_dp // LANES
    def middle(k, takes):
        size, at = chunks[k], offsets[k]
        slice_spec = pl.BlockSpec((2, 1, span, rows), lambda i, me: (0, i, 0, 0))
        flops = 12 * size * MIDDLE * BLOCK_HID * rows
        return pl.pallas_call(
            functools.partial(middle_kernel, ways, n_dp, scale),
            grid_spec=pltpu.PrefetchScalarGridSpec(
                num_scalar_prefetch=1,
                grid=(size,),
                in_specs=[slice_spec] * ways
                + [
                    pl.BlockSpec((1, MIDDLE, BLOCK_HID), lambda i, me, at=at: (i + at, 0, 0)),
                    pl.BlockSpec((1, BLOCK_HID, MIDDLE), lambda i, me, at=at: (i + at, 0, 0)),
                ],
                out_specs=[slice_spec] * ways
                + [pl.BlockSpec((n_dp, 1, share, LANES), lambda i, me: (0, i, 0, 0))],
                scratch_shapes=[pltpu.VMEM((MIDDLE, rows), BF16)] * 4,
            ),
            out_shape=[pltpu.HBM((2, size, span, rows), BF16)] * ways
            + [pltpu.HBM((n_dp, size, share, LANES), BF16)],
            compiler_params=params(),
            cost_estimate=cost(flops, size * MIDDLE * (8 * rows + 8 * BLOCK_HID)),
            name="middle",
        )(me, *in_hbm(takes), left_one, right_two)

    def summed(grads):
        return lax.psum_scatter(grads, "dp", scatter_dimension=0, tiled=True)

    queue = [dict(enumerate(sends[k * ways : (k + 1) * ways])) for k in range(n_parts)]
    got = [{0: parts[0]} for parts in queue]
    got[0].update(permute(queue[0], range(1, ways)))
    middles, big_sums = [], []
    for k in range(n_parts):
        parts = queue[k + 1] if k + 1 < n_parts else dict(enumerate(middles[0][:ways]))
        if k + 1 == n_parts:
            got.append({0: parts[0]})
        takes, ahead = lax.optimization_barrier((got[k], {m: parts[m] for m in early}))
        outs = middle(k, [takes[m] for m in range(ways)])
        ahead = permute(ahead, early)
        ahead, outs = lax.optimization_barrier((ahead, tuple(outs)))
        rest = after({m: parts[m] for m in late}, ahead)
        got[k + 1].update(ahead)
        got[k + 1].update(permute(rest, late))
        middles.append(outs)
        big_sums.append(summed(outs[ways]))
    returned = [got[n_parts]]
    for k in range(1, n_parts):
        parts = dict(enumerate(middles[k][:ways]))
        parts, _ = lax.optimization_barrier((parts, big_sums[k - 1]))
        before = returned[-1]
        taken = {0: parts[0]}
        for m in range(1, ways):
            taken.update(permute({m: after(parts[m], before[m])}, [m]))
        returned.append(taken)
    returned = [[taken[m] for m in range(ways)] for taken in returned]

    small_share = 2 * MIDDLE * BLOCK_IN // n_dp // LANES
    grad_tokens, small_grads = pl.pallas_call(
        functools.partial(last_kernel, chunks, ways, n_dp, scale),
        grid_spec=pltpu.PrefetchScalarGridSpec(
            num_scalar_prefetch=1,
            grid=(n_groups,),
            in_specs=[token_spec, token_spec, right_spec] + part_specs,
            out_specs=[
                token_spec,
                pl.BlockSpec((n_dp, GROUP, small_share, LANES), lambda i, me: (0, i, 0, 0)),
            ],
            scratch_shapes=[pltpu.VMEM((2, GROUP, MIDDLE, rows), BF16)],
        ),
        out_shape=[
            jax.ShapeDtypeStruct(tokens.shape, BF16),
            pltpu.HBM((n_dp, here, small_share, LANES), BF16),
        ],
        compiler_params=params(),
        cost_estimate=cost(moved * BLOCK_IN * 6, 2 * moved),
        name="last",
    )(me, tokens, cotangent, right_one, *in_hbm([part for parts in returned for part in parts]))
    small_grads, _ = lax.optimization_barrier((small_grads, big_sums[-1]))
    small_sum = summed(small_grads)

    big_shapes = ((BLOCK_HID // n_dp, MIDDLE), (MIDDLE // n_dp, BLOCK_HID))
    big = ()
    for k, size in enumerate(chunks):
        big = widen(big_sums[k], big_shapes, here, offsets[k], big, 1)
    grad_right_two, grad_left_one = big
    small_shapes = ((MIDDLE // n_dp, BLOCK_IN), (BLOCK_IN // n_dp, MIDDLE))
    grad_left_two, grad_right_one = widen(small_sum, small_shapes, here, 0, (), GROUP)
    return (
        grad_tokens,
        grad_right_one,
        grad_left_one,
        grad_right_two,
        grad_left_two,
        new_moment_one,
        new_moment_two,
        adam_update,
    )


def gelu_tanh(values):
    return jax.nn.gelu(values, approximate=True)


def on_device_plain(
    tokens, cotangent, right_one, left_one, right_two, left_two, grad_prev, moment_one, moment_two
):
    f32 = jnp.float32
    bf16 = jnp.bfloat16
    row_count = tokens.shape[0]
    blocks_here = right_one.shape[0]
    loss_scale = float(lax.axis_size("dp") * row_count) ** (-0.5)
    new_moment_one = 0.9 * moment_one + 0.1 * grad_prev
    new_moment_two = 0.95 * moment_two + 0.05 * grad_prev * grad_prev
    first_hat = new_moment_one / (1.0 - 0.9**10)
    second_hat = new_moment_two / (1.0 - 0.95**10)
    adam_update = first_hat / (jnp.sqrt(second_hat) + 1e-08)
    token_blocks = tokens.reshape(row_count, blocks_here, BLOCK_IN)
    first_mid = jnp.einsum(
        "tbk,bkj->bjt", token_blocks, right_one, preferred_element_type=f32
    ).astype(bf16)
    first_in = lax.all_to_all(
        first_mid.reshape(blocks_here, BLOCKS, SPLIT, row_count),
        "block",
        split_axis=1,
        concat_axis=0,
        tiled=True,
    )
    left_first = left_one.reshape(blocks_here, BLOCKS, SPLIT, BLOCK_HID)
    hidden_pre = jnp.einsum("bcqt,cbqf->cft", first_in, left_first, preferred_element_type=f32)
    hidden = gelu_tanh(hidden_pre).astype(bf16)
    second_mid = jnp.einsum("cft,cfj->cjt", hidden, right_two, preferred_element_type=f32).astype(
        bf16
    )
    second_in = lax.all_to_all(
        second_mid.reshape(blocks_here, BLOCKS, SPLIT, row_count),
        "block",
        split_axis=1,
        concat_axis=0,
        tiled=True,
    )
    left_second = left_two.reshape(blocks_here, BLOCKS, SPLIT, BLOCK_IN)
    grad_blocks = cotangent.reshape(row_count, blocks_here, BLOCK_IN)
    grad_second_out = jnp.einsum(
        "tdk,dcqk->cdqt", grad_blocks, left_second, preferred_element_type=f32
    ).astype(bf16)
    grad_left_two = (
        jnp.einsum("cdqt,tdk->dcqk", second_in, grad_blocks, preferred_element_type=f32)
        * loss_scale
    )
    grad_left_two = grad_left_two.reshape(blocks_here, MIDDLE, BLOCK_IN)
    grad_second = lax.all_to_all(grad_second_out, "block", split_axis=0, concat_axis=1, tiled=True)
    grad_second = grad_second.reshape(blocks_here, MIDDLE, row_count)
    grad_right_two = (
        jnp.einsum("cft,cjt->cfj", hidden, grad_second, preferred_element_type=f32) * loss_scale
    )
    grad_hidden = jnp.einsum("cjt,cfj->cft", grad_second, right_two, preferred_element_type=f32)
    unused_value, back_gelu = jax.vjp(gelu_tanh, hidden_pre)
    grad_pre = back_gelu(grad_hidden)[0].astype(bf16)
    grad_left_one = (
        jnp.einsum("bcqt,cft->cbqf", first_in, grad_pre, preferred_element_type=f32) * loss_scale
    )
    grad_left_one = grad_left_one.reshape(blocks_here, MIDDLE, BLOCK_HID)
    grad_first_out = jnp.einsum(
        "cft,cbqf->bcqt", grad_pre, left_first, preferred_element_type=f32
    ).astype(bf16)
    grad_first = lax.all_to_all(grad_first_out, "block", split_axis=0, concat_axis=1, tiled=True)
    grad_first = grad_first.reshape(blocks_here, MIDDLE, row_count)
    grad_right_one = (
        jnp.einsum("tbk,bjt->bkj", token_blocks, grad_first, preferred_element_type=f32)
        * loss_scale
    )
    grad_inputs = jnp.einsum(
        "bjt,bkj->tbk", grad_first, right_one, preferred_element_type=f32
    ).astype(bf16)
    grad_tokens = grad_inputs.reshape(row_count, blocks_here * BLOCK_IN)
    sum_right_one, sum_left_one, sum_right_two, sum_left_two = (
        lax.psum_scatter(
            grad_right_one.astype(jnp.bfloat16), "dp", scatter_dimension=1, tiled=True
        ).astype(jnp.float32),
        lax.psum_scatter(
            grad_left_one.astype(jnp.bfloat16), "dp", scatter_dimension=1, tiled=True
        ).astype(jnp.float32),
        lax.psum_scatter(
            grad_right_two.astype(jnp.bfloat16), "dp", scatter_dimension=1, tiled=True
        ).astype(jnp.float32),
        lax.psum_scatter(
            grad_left_two.astype(jnp.bfloat16), "dp", scatter_dimension=1, tiled=True
        ).astype(jnp.float32),
    )
    return (
        grad_tokens,
        sum_right_one,
        sum_left_one,
        sum_right_two,
        sum_left_two,
        new_moment_one,
        new_moment_two,
        adam_update,
    )


def solution(mesh):
    in_specs = (
        P("dp", "block"),
        P("dp", "block"),
        P("block", None, None),
        P("block", None, None),
        P("block", None, None),
        P("block", None, None),
        P("block", "dp"),
        P("block", "dp"),
        P("block", "dp"),
    )
    out_specs = (
        P("dp", "block"),
        P("block", "dp", None),
        P("block", "dp", None),
        P("block", "dp", None),
        P("block", "dp", None),
        P("block", "dp"),
        P("block", "dp"),
        P("block", "dp"),
    )
    here = BLOCKS // mesh.shape["block"]
    ways = mesh.shape["block"]
    fits = here % sum(CHUNKS) == 0 and here % GROUP == 0 and ways & (ways - 1) == 0
    return jax.shard_map(
        on_device_fast if fits else on_device_plain, mesh=mesh, in_specs=in_specs, out_specs=out_specs, check_vma=False
    )
```

```python
import functools
import math

import jax
import jax.numpy as jnp
import numpy as np
from jax import lax
from jax.experimental import pallas as pl
from jax.experimental.pallas import tpu as pltpu
from jax.sharding import PartitionSpec as P

BLOCKS = 96
SPLIT = 4
BLOCK_IN = 128
BLOCK_HID = 512
MIDDLE = 384

F32 = jnp.float32
BF16 = jnp.bfloat16
GROUP = 4
LANES = 128
VMEM_LIMIT = 62 * 1024 * 1024
CHUNKS = (2, 4, 6)


def dot(lhs, rhs, lhs_dim, rhs_dim):
    return lax.dot_general(
        lhs, rhs, (((lhs_dim,), (rhs_dim,)), ((), ())), preferred_element_type=F32
    )


def one_hot(source, width):
    return jnp.asarray(np.asarray(source)[:, None] == np.arange(width), dtype=BF16)


def permutation(outer, inner):
    rows = np.arange(inner * outer * SPLIT).reshape(inner, outer, SPLIT)
    return one_hot(rows.transpose(1, 0, 2).reshape(-1), rows.size)


def first_kernel(chunks, ways, me_ref, x_ref, g_ref, right_ref, left_ref, perm_ref, *refs):
    outs, (rows,) = refs[:-1], refs[-1:]
    here = sum(chunks)
    span = here * SPLIT
    perm = perm_ref[...]
    for which in range(2):
        for b in range(GROUP):
            lanes = slice(b * BLOCK_IN, (b + 1) * BLOCK_IN)
            if which == 0:
                value = dot(right_ref[b], x_ref[:, lanes], 0, 1)
            else:
                value = dot(left_ref[b], g_ref[:, lanes], 1, 1)
            rows[which, b] = value.astype(BF16)
        for m in range(ways):
            start = pl.multiple_of((me_ref[0] ^ m) * span, 16)
            taken = jnp.concatenate(
                [rows[which, b, pl.ds(start, span), :] for b in range(GROUP)], axis=0
            )
            mixed = dot(perm, taken, 1, 0).astype(BF16)
            at = chunks[0]
            for k, size in enumerate(chunks[1:]):
                part = mixed[at * GROUP * SPLIT : (at + size) * GROUP * SPLIT]
                outs[k * ways + m][which] = part.reshape(size, GROUP * SPLIT, part.shape[-1])
                at += size


def lead_kernel(size, ways, me_ref, x_ref, g_ref, right_ref, left_ref, perm_ref, pick_ref, *refs):
    outs, rows = refs[:-1], refs[-1]
    perm = perm_ref[...]
    pick = pick_ref[...]
    right = right_ref[...].reshape(GROUP * BLOCK_IN, MIDDLE)
    right = dot(right, pick, 1, 1).astype(BF16)
    left = [dot(pick, left_ref[b], 1, 0).astype(BF16) for b in range(GROUP)]
    for which in range(2):
        values = []
        for b in range(GROUP):
            lanes = slice(b * BLOCK_IN, (b + 1) * BLOCK_IN)
            if which == 0:
                value = dot(right[lanes], x_ref[:, lanes], 0, 1)
            else:
                value = dot(left[b], g_ref[:, lanes], 1, 1)
            values.append(value.astype(BF16))
        rows[...] = dot(perm, jnp.concatenate(values, axis=0), 1, 0).astype(BF16)
        tall = size * GROUP * SPLIT
        for m in range(ways):
            start = pl.multiple_of((me_ref[0] ^ m) * tall, 16)
            part = rows[pl.ds(start, tall), :]
            outs[m][which] = part.reshape(size, GROUP * SPLIT, part.shape[-1])


def middle_kernel(ways, n_old, n_dp, scale, me_ref, *refs):
    takes = refs[:ways]
    left_ref, right_ref = refs[ways : ways + 2]
    refs = refs[ways + 2 + n_old :]
    gives = refs[:ways]
    grads_ref, first_in, grad_in, second_out, grad_out = refs[ways:]
    span = MIDDLE // ways
    for m in range(ways):
        start = pl.multiple_of((me_ref[0] ^ m) * span, 16)
        first_in[pl.ds(start, span), :] = takes[m][0, 0]
        grad_in[pl.ds(start, span), :] = takes[m][1, 0]
    left = left_ref[0]
    right = right_ref[0]
    pre = dot(left, first_in[...], 0, 0)
    root = math.sqrt(2.0 / math.pi)
    square = pre * pre
    bend = jnp.tanh(root * (pre + 0.044715 * (square * pre)))
    half = 0.5 * (1.0 + bend)
    hidden = (pre * half).astype(BF16)
    slope = half + 0.5 * pre * (1.0 - bend * bend) * (root * (1.0 + 3 * 0.044715 * square))
    second_out[...] = dot(right, hidden, 0, 0).astype(BF16)
    grad_second = grad_in[...]
    grad_pre = (dot(right, grad_second, 1, 0) * slope).astype(BF16)
    grad_out[...] = dot(left, grad_pre, 1, 0).astype(BF16)
    for m in range(ways):
        start = pl.multiple_of((me_ref[0] ^ m) * span, 16)
        gives[m][0, 0] = second_out[pl.ds(start, span), :]
        gives[m][1, 0] = grad_out[pl.ds(start, span), :]
    grad_right = (dot(hidden, grad_second, 1, 1) * scale).astype(BF16)
    grad_left = (dot(first_in[...], grad_pre, 1, 1) * scale).astype(BF16)
    at = 0
    for grad in (grad_right, grad_left):
        depth = grad.shape[0] // n_dp
        for lane in range(0, grad.shape[1], LANES):
            for z in range(n_dp):
                grads_ref[z, 0, at : at + depth, :] = grad[
                    z * depth : (z + 1) * depth, lane : lane + LANES
                ]
            at += depth


def last_kernel(chunks, ways, n_dp, scale, me_ref, x_ref, g_ref, right_ref, perm_ref, *refs):
    count = len(chunks) * ways
    takes = refs[:count]
    tokens_ref, grads_ref, rows = refs[count:]
    here = sum(chunks)
    span = here * SPLIT
    perm = perm_ref[...]
    for which in range(2):
        for m in range(ways):
            start = pl.multiple_of((me_ref[0] ^ m) * span, 16)
            taken = jnp.concatenate(
                [
                    takes[k * ways + m][which].reshape(size * GROUP * SPLIT, -1)
                    for k, size in enumerate(chunks)
                ],
                axis=0,
            )
            mixed = dot(perm, taken, 1, 0).astype(BF16)
            for b in range(GROUP):
                rows[which, b, pl.ds(start, span), :] = mixed[b * span : (b + 1) * span]
    for b in range(GROUP):
        lanes = slice(b * BLOCK_IN, (b + 1) * BLOCK_IN)
        second_in = rows[0, b]
        grad_first = rows[1, b]
        tokens_ref[:, lanes] = dot(grad_first, right_ref[b], 0, 1).astype(BF16)
        grad_left = (dot(second_in, g_ref[:, lanes], 1, 0) * scale).astype(BF16)
        grad_right = (dot(x_ref[:, lanes], grad_first, 0, 1) * scale).astype(BF16)
        at = 0
        for grad in (grad_left, grad_right):
            depth = grad.shape[0] // n_dp
            for lane in range(0, grad.shape[1], LANES):
                for z in range(n_dp):
                    grads_ref[z, b, at : at + depth, :] = grad[
                        z * depth : (z + 1) * depth, lane : lane + LANES
                    ]
                at += depth


def widen_kernel(n_old, sum_ref, *refs):
    at = 0
    for out_ref in refs[n_old:]:
        depth, width = out_ref.shape[1:]
        for lane in range(0, width, LANES):
            out_ref[:, :, lane : lane + LANES] = sum_ref[0, :, at : at + depth, :].astype(F32)
            at += depth


def in_hbm(arrays):
    return [pltpu.with_memory_space_constraint(array, pltpu.HBM) for array in arrays]


def params():
    return pltpu.CompilerParams(vmem_limit_bytes=VMEM_LIMIT)


def cost(flops, moved, transcendentals=0):
    return pl.CostEstimate(
        flops=int(flops), bytes_accessed=int(moved), transcendentals=int(transcendentals)
    )


def widen(summed, shapes, here, first_block, old, per_step):
    size, depth, _ = summed.shape[1:]
    n_old = len(old)
    any_spec = pl.BlockSpec(memory_space=pl.ANY)
    at = first_block // per_step
    return pl.pallas_call(
        functools.partial(widen_kernel, n_old),
        grid=(size // per_step,),
        in_specs=[pl.BlockSpec((1, per_step, depth, LANES), lambda i: (0, i, 0, 0))]
        + [any_spec] * n_old,
        out_specs=[
            pl.BlockSpec((per_step,) + tuple(shape), lambda i, at=at: (i + at, 0, 0))
            for shape in shapes
        ],
        out_shape=[jax.ShapeDtypeStruct((here,) + tuple(shape), F32) for shape in shapes],
        input_output_aliases={i + 1: i for i in range(n_old)},
        compiler_params=params(),
        cost_estimate=cost(0, summed.size * 6),
        name="widen",
    )(summed, *old)


def on_device_fast(
    tokens, cotangent, right_one, left_one, right_two, left_two, grad_prev, moment_one, moment_two
):
    rows = tokens.shape[0]
    here = right_one.shape[0]
    ways = lax.axis_size("block")
    n_dp = lax.axis_size("dp")
    span = here * SPLIT
    scale = float(n_dp * rows) ** (-0.5)
    me = lax.axis_index("block").astype(jnp.int32).reshape(1)
    unit = here // sum(CHUNKS)
    chunks = tuple(size * unit for size in CHUNKS)
    n_groups = here // GROUP
    tile = GROUP * SPLIT
    wide = GROUP * BLOCK_IN

    new_moment_one = 0.9 * moment_one + 0.1 * grad_prev
    new_moment_two = 0.95 * moment_two + 0.05 * grad_prev * grad_prev
    first_hat = new_moment_one / (1.0 - 0.9**10)
    second_hat = new_moment_two / (1.0 - 0.95**10)
    adam_update = first_hat / (jnp.sqrt(second_hat) + 1e-08)

    token_spec = pl.BlockSpec((rows, wide), lambda i, me: (0, i))
    right_spec = pl.BlockSpec((GROUP, BLOCK_IN, MIDDLE), lambda i, me: (i, 0, 0))
    left_spec = pl.BlockSpec((GROUP, MIDDLE, BLOCK_IN), lambda i, me: (i, 0, 0))
    part_specs = [
        pl.BlockSpec((2, size, tile, rows), lambda i, me: (0, 0, i, 0))
        for size in chunks
        for _ in range(ways)
    ]
    part_shapes = [
        pltpu.HBM((2, size, span, rows), BF16) for size in chunks for _ in range(ways)
    ]
    moved = 2 * here * MIDDLE * rows
    first_in_specs = [token_spec, token_spec, right_spec, left_spec]
    lead_perm = permutation(ways * chunks[0], GROUP)
    lead_rows = np.arange(MIDDLE).reshape(ways, here, SPLIT)[:, : chunks[0]]
    lead_pick = one_hot(lead_rows.reshape(-1), MIDDLE)

    def whole(array):
        return pl.BlockSpec(array.shape, lambda i, me: (0, 0))

    perm = permutation(here, GROUP)
    perm_back = permutation(GROUP, here)
    lead = pl.pallas_call(
        functools.partial(lead_kernel, chunks[0], ways),
        grid_spec=pltpu.PrefetchScalarGridSpec(
            num_scalar_prefetch=1,
            grid=(n_groups,),
            in_specs=first_in_specs + [whole(lead_perm), whole(lead_pick)],
            out_specs=part_specs[:ways],
            scratch_shapes=[pltpu.VMEM((ways * chunks[0] * tile, rows), BF16)],
        ),
        out_shape=part_shapes[:ways],
        compiler_params=params(),
        cost_estimate=cost(moved * BLOCK_IN * chunks[0] / here * 5, moved),
        name="lead",
    )(me, tokens, cotangent, right_one, left_two, lead_perm, lead_pick)

    lane_done = {}

    def send(parts, m):
        part = parts[m]
        if m // 2 in lane_done:
            part, _ = lax.optimization_barrier((part, lane_done[m // 2]))
        taken = lax.ppermute(part, "block", [(i, i ^ m) for i in range(ways)])
        lane_done[m // 2] = taken
        return taken

    def send_all(parts, ms):
        return {m: send(parts, m) for m in ms}

    evens = list(range(2, ways, 2))
    odds = list(range(1, ways, 2))
    near = [m for m in range(2, ways) if (m // 2) & (m // 2 - 1) == 0]
    everyone = evens + odds
    offsets = [sum(chunks[:k]) for k in range(len(chunks))]
    n_parts = len(chunks)

    share = (BLOCK_HID * MIDDLE + MIDDLE * BLOCK_HID) // n_dp // LANES
    def middle(k, takes, old, first_give, n_give):
        size, at = chunks[k], offsets[k]
        slice_spec = pl.BlockSpec((2, 1, span, rows), lambda i, me: (0, i, 0, 0))
        give_spec = pl.BlockSpec((2, 1, span, rows), lambda i, me: (0, i + first_give, 0, 0))
        flops = 12 * size * MIDDLE * BLOCK_HID * rows
        return pl.pallas_call(
            functools.partial(middle_kernel, ways, len(old), n_dp, scale),
            grid_spec=pltpu.PrefetchScalarGridSpec(
                num_scalar_prefetch=1,
                grid=(size,),
                in_specs=[slice_spec] * ways
                + [
                    pl.BlockSpec((1, MIDDLE, BLOCK_HID), lambda i, me: (i + at, 0, 0)),
                    pl.BlockSpec((1, BLOCK_HID, MIDDLE), lambda i, me: (i + at, 0, 0)),
                ]
                + [pl.BlockSpec(memory_space=pl.ANY)] * len(old),
                out_specs=[give_spec] * ways
                + [pl.BlockSpec((n_dp, 1, share, LANES), lambda i, me: (0, i, 0, 0))],
                scratch_shapes=[pltpu.VMEM((MIDDLE, rows), BF16)] * 4,
            ),
            out_shape=[pltpu.HBM((2, n_give, span, rows), BF16)] * ways
            + [pltpu.HBM((n_dp, size, share, LANES), BF16)],
            input_output_aliases={ways + 3 + i: i for i in range(len(old))},
            compiler_params=params(),
            cost_estimate=cost(flops, size * MIDDLE * (8 * rows + 8 * BLOCK_HID)),
            name="middle",
        )(me, *in_hbm(takes), left_one, right_two, *in_hbm(old))

    def summed(grads):
        return lax.psum_scatter(grads, "dp", scatter_dimension=0, tiled=True)

    queue = [dict(enumerate(lead))]
    got = [{0: lead[0]}]
    for m in near + [m for m in everyone if m not in near]:
        got[0][m] = lax.ppermute(lead[m], "block", [(i, i ^ m) for i in range(ways)])
        lane_done[m // 2] = got[0][m]
    rest = pl.pallas_call(
        functools.partial(first_kernel, chunks, ways),
        grid_spec=pltpu.PrefetchScalarGridSpec(
            num_scalar_prefetch=1,
            grid=(n_groups,),
            in_specs=first_in_specs + [whole(perm)],
            out_specs=part_specs[ways:],
            scratch_shapes=[pltpu.VMEM((2, GROUP, MIDDLE, rows), BF16)],
        ),
        out_shape=part_shapes[ways:],
        compiler_params=params(),
        cost_estimate=cost(moved * BLOCK_IN * 5, 2 * moved),
        name="first",
    )(me, tokens, cotangent, right_one, left_two, perm)
    for k in range(n_parts - 1):
        queue.append(dict(enumerate(rest[k * ways : (k + 1) * ways])))

    early_size = offsets[-1]
    back_chunks = (early_size, chunks[-1])
    big_sums, early, held = [], (), {}
    for k in range(n_parts):
        last_part = k + 1 == n_parts
        if last_part:
            parts = dict(enumerate(early))
            ahead = send_all(parts, [m for m in near if m % 2 == 0] + [m for m in near if m % 2])
            outs = middle(k, [got[k][m] for m in range(ways)], (), 0, chunks[-1])
        else:
            parts = queue[k + 1]
            ahead = send_all(parts, [m for m in near if m % 2 == 0])
            outs = middle(k, [got[k][m] for m in range(ways)], early, offsets[k], early_size)
        held, outs = lax.optimization_barrier((ahead, tuple(outs)))
        big_sums.append(summed(outs[ways]))
        parts = lax.optimization_barrier((parts, held))[0]
        if last_part:
            late = dict(enumerate(outs[:ways]))
        else:
            early = outs[:ways]
            got.append({0: parts[0]} | held | send_all(parts, [m for m in everyone if m not in held]))
    early = parts
    late = lax.optimization_barrier((late, tuple(big_sums[:-1])))[0]
    back = [{0: early[0]} | held, {0: late[0]}]
    far = [m for m in everyone if m > 1 and m not in near]
    for m in far + [1]:
        back[0][m] = lax.ppermute(early[m], "block", [(i, i ^ m) for i in range(ways)])
    evens_near = [m for m in near if m % 2 == 0]
    odds_near = [m for m in near if m % 2]
    for m in evens_near:
        back[1][m] = lax.ppermute(late[m], "block", [(i, i ^ m) for i in range(ways)])
    waits = [(m, back[0][far[i % len(far)]]) for i, m in enumerate(odds_near)]
    waits += [(m, back[1][evens_near[i % len(evens_near)]]) for i, m in enumerate(far)]
    for m, done in waits + [(1, back[0][1])]:
        part, _ = lax.optimization_barrier((late[m], done))
        back[1][m] = lax.ppermute(part, "block", [(i, i ^ m) for i in range(ways)])
    returned = [[taken[m] for m in range(ways)] for taken in back]
    back_specs = [
        pl.BlockSpec((2, size, tile, rows), lambda i, me: (0, 0, i, 0))
        for size in back_chunks
        for _ in range(ways)
    ]

    small_share = 2 * MIDDLE * BLOCK_IN // n_dp // LANES
    grad_tokens, small_grads = pl.pallas_call(
        functools.partial(last_kernel, back_chunks, ways, n_dp, scale),
        grid_spec=pltpu.PrefetchScalarGridSpec(
            num_scalar_prefetch=1,
            grid=(n_groups,),
            in_specs=[token_spec, token_spec, right_spec, whole(perm_back)] + back_specs,
            out_specs=[
                token_spec,
                pl.BlockSpec((n_dp, GROUP, small_share, LANES), lambda i, me: (0, i, 0, 0)),
            ],
            scratch_shapes=[pltpu.VMEM((2, GROUP, MIDDLE, rows), BF16)],
        ),
        out_shape=[
            jax.ShapeDtypeStruct(tokens.shape, BF16),
            pltpu.HBM((n_dp, here, small_share, LANES), BF16),
        ],
        compiler_params=params(),
        cost_estimate=cost(moved * BLOCK_IN * 6, 2 * moved),
        name="last",
    )(me, tokens, cotangent, right_one, perm_back, *in_hbm([part for parts in returned for part in parts]))
    small_grads, _ = lax.optimization_barrier((small_grads, big_sums[-1]))
    small_sum = summed(small_grads)

    big_shapes = ((BLOCK_HID // n_dp, MIDDLE), (MIDDLE // n_dp, BLOCK_HID))
    big = ()
    for k, size in enumerate(chunks):
        big = widen(big_sums[k], big_shapes, here, offsets[k], big, 1)
    grad_right_two, grad_left_one = big
    small_shapes = ((MIDDLE // n_dp, BLOCK_IN), (BLOCK_IN // n_dp, MIDDLE))
    grad_left_two, grad_right_one = widen(small_sum, small_shapes, here, 0, (), GROUP)
    return (
        grad_tokens,
        grad_right_one,
        grad_left_one,
        grad_right_two,
        grad_left_two,
        new_moment_one,
        new_moment_two,
        adam_update,
    )


def gelu_tanh(values):
    return jax.nn.gelu(values, approximate=True)


def on_device_plain(
    tokens, cotangent, right_one, left_one, right_two, left_two, grad_prev, moment_one, moment_two
):
    f32 = jnp.float32
    bf16 = jnp.bfloat16
    row_count = tokens.shape[0]
    blocks_here = right_one.shape[0]
    loss_scale = float(lax.axis_size("dp") * row_count) ** (-0.5)
    new_moment_one = 0.9 * moment_one + 0.1 * grad_prev
    new_moment_two = 0.95 * moment_two + 0.05 * grad_prev * grad_prev
    first_hat = new_moment_one / (1.0 - 0.9**10)
    second_hat = new_moment_two / (1.0 - 0.95**10)
    adam_update = first_hat / (jnp.sqrt(second_hat) + 1e-08)
    token_blocks = tokens.reshape(row_count, blocks_here, BLOCK_IN)
    first_mid = jnp.einsum(
        "tbk,bkj->bjt", token_blocks, right_one, preferred_element_type=f32
    ).astype(bf16)
    first_in = lax.all_to_all(
        first_mid.reshape(blocks_here, BLOCKS, SPLIT, row_count),
        "block",
        split_axis=1,
        concat_axis=0,
        tiled=True,
    )
    left_first = left_one.reshape(blocks_here, BLOCKS, SPLIT, BLOCK_HID)
    hidden_pre = jnp.einsum("bcqt,cbqf->cft", first_in, left_first, preferred_element_type=f32)
    hidden = gelu_tanh(hidden_pre).astype(bf16)
    second_mid = jnp.einsum("cft,cfj->cjt", hidden, right_two, preferred_element_type=f32).astype(
        bf16
    )
    second_in = lax.all_to_all(
        second_mid.reshape(blocks_here, BLOCKS, SPLIT, row_count),
        "block",
        split_axis=1,
        concat_axis=0,
        tiled=True,
    )
    left_second = left_two.reshape(blocks_here, BLOCKS, SPLIT, BLOCK_IN)
    grad_blocks = cotangent.reshape(row_count, blocks_here, BLOCK_IN)
    grad_second_out = jnp.einsum(
        "tdk,dcqk->cdqt", grad_blocks, left_second, preferred_element_type=f32
    ).astype(bf16)
    grad_left_two = (
        jnp.einsum("cdqt,tdk->dcqk", second_in, grad_blocks, preferred_element_type=f32)
        * loss_scale
    )
    grad_left_two = grad_left_two.reshape(blocks_here, MIDDLE, BLOCK_IN)
    grad_second = lax.all_to_all(grad_second_out, "block", split_axis=0, concat_axis=1, tiled=True)
    grad_second = grad_second.reshape(blocks_here, MIDDLE, row_count)
    grad_right_two = (
        jnp.einsum("cft,cjt->cfj", hidden, grad_second, preferred_element_type=f32) * loss_scale
    )
    grad_hidden = jnp.einsum("cjt,cfj->cft", grad_second, right_two, preferred_element_type=f32)
    unused_value, back_gelu = jax.vjp(gelu_tanh, hidden_pre)
    grad_pre = back_gelu(grad_hidden)[0].astype(bf16)
    grad_left_one = (
        jnp.einsum("bcqt,cft->cbqf", first_in, grad_pre, preferred_element_type=f32) * loss_scale
    )
    grad_left_one = grad_left_one.reshape(blocks_here, MIDDLE, BLOCK_HID)
    grad_first_out = jnp.einsum(
        "cft,cbqf->bcqt", grad_pre, left_first, preferred_element_type=f32
    ).astype(bf16)
    grad_first = lax.all_to_all(grad_first_out, "block", split_axis=0, concat_axis=1, tiled=True)
    grad_first = grad_first.reshape(blocks_here, MIDDLE, row_count)
    grad_right_one = (
        jnp.einsum("tbk,bjt->bkj", token_blocks, grad_first, preferred_element_type=f32)
        * loss_scale
    )
    grad_inputs = jnp.einsum(
        "bjt,bkj->tbk", grad_first, right_one, preferred_element_type=f32
    ).astype(bf16)
    grad_tokens = grad_inputs.reshape(row_count, blocks_here * BLOCK_IN)
    sum_right_one, sum_left_one, sum_right_two, sum_left_two = (
        lax.psum_scatter(
            grad_right_one.astype(jnp.bfloat16), "dp", scatter_dimension=1, tiled=True
        ).astype(jnp.float32),
        lax.psum_scatter(
            grad_left_one.astype(jnp.bfloat16), "dp", scatter_dimension=1, tiled=True
        ).astype(jnp.float32),
        lax.psum_scatter(
            grad_right_two.astype(jnp.bfloat16), "dp", scatter_dimension=1, tiled=True
        ).astype(jnp.float32),
        lax.psum_scatter(
            grad_left_two.astype(jnp.bfloat16), "dp", scatter_dimension=1, tiled=True
        ).astype(jnp.float32),
    )
    return (
        grad_tokens,
        sum_right_one,
        sum_left_one,
        sum_right_two,
        sum_left_two,
        new_moment_one,
        new_moment_two,
        adam_update,
    )


def solution(mesh):
    in_specs = (
        P("dp", "block"),
        P("dp", "block"),
        P("block", None, None),
        P("block", None, None),
        P("block", None, None),
        P("block", None, None),
        P("block", "dp"),
        P("block", "dp"),
        P("block", "dp"),
    )
    out_specs = (
        P("dp", "block"),
        P("block", "dp", None),
        P("block", "dp", None),
        P("block", "dp", None),
        P("block", "dp", None),
        P("block", "dp"),
        P("block", "dp"),
        P("block", "dp"),
    )
    here = BLOCKS // mesh.shape["block"]
    ways = mesh.shape["block"]
    fits = here % sum(CHUNKS) == 0 and ways >= 8 and here % GROUP == 0 and ways & (ways - 1) == 0
    return jax.shard_map(
        on_device_fast if fits else on_device_plain, mesh=mesh, in_specs=in_specs, out_specs=out_specs, check_vma=False
    )
```

```python
import functools
import math

import jax
import jax.numpy as jnp
import numpy as np
from jax import lax
from jax.experimental import pallas as pl
from jax.experimental.pallas import tpu as pltpu
from jax.sharding import PartitionSpec as P

BLOCKS = 96
SPLIT = 4
BLOCK_IN = 128
BLOCK_HID = 512
MIDDLE = 384

F32 = jnp.float32
BF16 = jnp.bfloat16
GROUP = 4
LANES = 128
VMEM_LIMIT = 65000 * 1024
CHUNKS = (2, 4, 6)


def dot(lhs, rhs, lhs_dim, rhs_dim):
    return lax.dot_general(
        lhs, rhs, (((lhs_dim,), (rhs_dim,)), ((), ())), preferred_element_type=F32
    )


def one_hot(source, width):
    return jnp.asarray(np.asarray(source)[:, None] == np.arange(width), dtype=BF16)


def permutation(outer, inner):
    rows = np.arange(inner * outer * SPLIT).reshape(inner, outer, SPLIT)
    return one_hot(rows.transpose(1, 0, 2).reshape(-1), rows.size)


def first_kernel(chunks, skip, ways, me_ref, x_ref, g_ref, right_ref, left_ref, perm_ref, *refs):
    outs, (rows,) = refs[:-1], refs[-1:]
    here = sum(chunks)
    span = here * SPLIT
    perm = perm_ref[...]
    for which in range(2):
        for b in range(GROUP):
            lanes = slice(b * BLOCK_IN, (b + 1) * BLOCK_IN)
            if which == 0:
                value = dot(right_ref[b], x_ref[:, lanes], 0, 1)
            else:
                value = dot(left_ref[b], g_ref[:, lanes], 1, 1)
            rows[which, b] = value.astype(BF16)
        for m in range(ways):
            start = pl.multiple_of((me_ref[0] ^ m) * span, 16)
            taken = jnp.concatenate(
                [rows[which, b, pl.ds(start, span), :] for b in range(GROUP)], axis=0
            )
            mixed = dot(perm, taken, 1, 0).astype(BF16)
            at = sum(chunks[:skip])
            for k, size in enumerate(chunks[skip:]):
                part = mixed[at * GROUP * SPLIT : (at + size) * GROUP * SPLIT]
                outs[k * ways + m][which] = part.reshape(size, GROUP * SPLIT, part.shape[-1])
                at += size


def lead_kernel(size, ways, me_ref, x_ref, g_ref, right_ref, left_ref, perm_ref, pick_ref, *refs):
    outs, rows = refs[:-1], refs[-1]
    perm = perm_ref[...]
    pick = pick_ref[...]
    right = right_ref[...].reshape(GROUP * BLOCK_IN, MIDDLE)
    right = dot(right, pick, 1, 1).astype(BF16)
    left = [dot(pick, left_ref[b], 1, 0).astype(BF16) for b in range(GROUP)]
    for which in range(2):
        values = []
        for b in range(GROUP):
            lanes = slice(b * BLOCK_IN, (b + 1) * BLOCK_IN)
            if which == 0:
                value = dot(right[lanes], x_ref[:, lanes], 0, 1)
            else:
                value = dot(left[b], g_ref[:, lanes], 1, 1)
            values.append(value.astype(BF16))
        rows[...] = dot(perm, jnp.concatenate(values, axis=0), 1, 0).astype(BF16)
        tall = size * GROUP * SPLIT
        for m in range(ways):
            start = pl.multiple_of((me_ref[0] ^ m) * tall, 16)
            part = rows[pl.ds(start, tall), :]
            outs[m][which] = part.reshape(size, GROUP * SPLIT, part.shape[-1])


def middle_kernel(ways, n_old, n_dp, scale, me_ref, *refs):
    takes = refs[:ways]
    left_ref, right_ref = refs[ways : ways + 2]
    refs = refs[ways + 2 + n_old :]
    gives = refs[:ways]
    grads_ref, first_in, grad_in, second_out, grad_out = refs[ways:]
    span = MIDDLE // ways
    for m in range(ways):
        start = pl.multiple_of((me_ref[0] ^ m) * span, 16)
        first_in[pl.ds(start, span), :] = takes[m][0, 0]
        grad_in[pl.ds(start, span), :] = takes[m][1, 0]
    left = left_ref[0]
    right = right_ref[0]
    pre = dot(left, first_in[...], 0, 0)
    root = math.sqrt(2.0 / math.pi)
    square = pre * pre
    bend = jnp.tanh(root * (pre + 0.044715 * (square * pre)))
    half = 0.5 * (1.0 + bend)
    hidden = (pre * half).astype(BF16)
    slope = half + 0.5 * pre * (1.0 - bend * bend) * (root * (1.0 + 3 * 0.044715 * square))
    second_out[...] = dot(right, hidden, 0, 0).astype(BF16)
    grad_second = grad_in[...]
    grad_pre = (dot(right, grad_second, 1, 0) * slope).astype(BF16)
    grad_out[...] = dot(left, grad_pre, 1, 0).astype(BF16)
    for m in range(ways):
        start = pl.multiple_of((me_ref[0] ^ m) * span, 16)
        gives[m][0, 0] = second_out[pl.ds(start, span), :]
        gives[m][1, 0] = grad_out[pl.ds(start, span), :]
    grad_right = (dot(hidden, grad_second, 1, 1) * scale).astype(BF16)
    grad_left = (dot(first_in[...], grad_pre, 1, 1) * scale).astype(BF16)
    at = 0
    for grad in (grad_right, grad_left):
        depth = grad.shape[0] // n_dp
        for lane in range(0, grad.shape[1], LANES):
            for z in range(n_dp):
                grads_ref[z, 0, at : at + depth, :] = grad[
                    z * depth : (z + 1) * depth, lane : lane + LANES
                ]
            at += depth


def last_kernel(chunks, ways, n_dp, scale, me_ref, x_ref, g_ref, right_ref, perm_ref, *refs):
    count = len(chunks) * ways
    takes = refs[:count]
    tokens_ref, grads_ref, rows = refs[count:]
    here = sum(chunks)
    span = here * SPLIT
    perm = perm_ref[...]
    for which in range(2):
        for m in range(ways):
            start = pl.multiple_of((me_ref[0] ^ m) * span, 16)
            taken = jnp.concatenate(
                [
                    takes[k * ways + m][which].reshape(size * GROUP * SPLIT, -1)
                    for k, size in enumerate(chunks)
                ],
                axis=0,
            )
            mixed = dot(perm, taken, 1, 0).astype(BF16)
            for b in range(GROUP):
                rows[which, b, pl.ds(start, span), :] = mixed[b * span : (b + 1) * span]
    for b in range(GROUP):
        lanes = slice(b * BLOCK_IN, (b + 1) * BLOCK_IN)
        second_in = rows[0, b]
        grad_first = rows[1, b]
        tokens_ref[:, lanes] = dot(grad_first, right_ref[b], 0, 1).astype(BF16)
        grad_left = (dot(second_in, g_ref[:, lanes], 1, 0) * scale).astype(BF16)
        grad_right = (dot(x_ref[:, lanes], grad_first, 0, 1) * scale).astype(BF16)
        at = 0
        for grad in (grad_left, grad_right):
            depth = grad.shape[0] // n_dp
            for lane in range(0, grad.shape[1], LANES):
                for z in range(n_dp):
                    grads_ref[z, b, at : at + depth, :] = grad[
                        z * depth : (z + 1) * depth, lane : lane + LANES
                    ]
                at += depth


def widen_kernel(n_old, sum_ref, *refs):
    at = 0
    for out_ref in refs[n_old:]:
        depth, width = out_ref.shape[1:]
        for lane in range(0, width, LANES):
            out_ref[:, :, lane : lane + LANES] = sum_ref[0, :, at : at + depth, :].astype(F32)
            at += depth


def in_hbm(arrays):
    return [pltpu.with_memory_space_constraint(array, pltpu.HBM) for array in arrays]


def params():
    return pltpu.CompilerParams(vmem_limit_bytes=VMEM_LIMIT)


def cost(flops, moved, transcendentals=0):
    return pl.CostEstimate(
        flops=int(flops), bytes_accessed=int(moved), transcendentals=int(transcendentals)
    )


def widen(summed, shapes, here, first_block, old, per_step):
    size, depth, _ = summed.shape[1:]
    n_old = len(old)
    any_spec = pl.BlockSpec(memory_space=pl.ANY)
    at = first_block // per_step
    return pl.pallas_call(
        functools.partial(widen_kernel, n_old),
        grid=(size // per_step,),
        in_specs=[pl.BlockSpec((1, per_step, depth, LANES), lambda i: (0, i, 0, 0))]
        + [any_spec] * n_old,
        out_specs=[
            pl.BlockSpec((per_step,) + tuple(shape), lambda i, at=at: (i + at, 0, 0))
            for shape in shapes
        ],
        out_shape=[jax.ShapeDtypeStruct((here,) + tuple(shape), F32) for shape in shapes],
        input_output_aliases={i + 1: i for i in range(n_old)},
        compiler_params=params(),
        cost_estimate=cost(0, summed.size * 6),
        name="widen",
    )(summed, *old)


def on_device_fast(
    tokens, cotangent, right_one, left_one, right_two, left_two, grad_prev, moment_one, moment_two
):
    rows = tokens.shape[0]
    here = right_one.shape[0]
    ways = lax.axis_size("block")
    n_dp = lax.axis_size("dp")
    span = here * SPLIT
    scale = float(n_dp * rows) ** (-0.5)
    me = lax.axis_index("block").astype(jnp.int32).reshape(1)
    unit = here // sum(CHUNKS)
    chunks = tuple(size * unit for size in CHUNKS)
    n_groups = here // GROUP
    tile = GROUP * SPLIT
    wide = GROUP * BLOCK_IN

    new_moment_one = 0.9 * moment_one + 0.1 * grad_prev
    new_moment_two = 0.95 * moment_two + 0.05 * grad_prev * grad_prev
    first_hat = new_moment_one / (1.0 - 0.9**10)
    second_hat = new_moment_two / (1.0 - 0.95**10)
    adam_update = first_hat / (jnp.sqrt(second_hat) + 1e-08)

    token_spec = pl.BlockSpec((rows, wide), lambda i, me: (0, i))
    right_spec = pl.BlockSpec((GROUP, BLOCK_IN, MIDDLE), lambda i, me: (i, 0, 0))
    left_spec = pl.BlockSpec((GROUP, MIDDLE, BLOCK_IN), lambda i, me: (i, 0, 0))
    part_specs = [
        pl.BlockSpec((2, size, tile, rows), lambda i, me: (0, 0, i, 0))
        for size in chunks
        for _ in range(ways)
    ]
    part_shapes = [
        pltpu.HBM((2, size, span, rows), BF16) for size in chunks for _ in range(ways)
    ]
    moved = 2 * here * MIDDLE * rows
    offsets = [sum(chunks[:k]) for k in range(len(chunks))]
    n_parts = len(chunks)
    first_in_specs = [token_spec, token_spec, right_spec, left_spec]

    def whole(array):
        return pl.BlockSpec(array.shape, lambda i, me: (0, 0))

    perm = permutation(here, GROUP)
    perm_back = permutation(GROUP, here)
    def lead(k):
        size, at = chunks[k], offsets[k]
        mix = permutation(ways * size, GROUP)
        pick = np.arange(MIDDLE).reshape(ways, here, SPLIT)[:, at : at + size]
        pick = one_hot(pick.reshape(-1), MIDDLE)
        return pl.pallas_call(
            functools.partial(lead_kernel, size, ways),
            grid_spec=pltpu.PrefetchScalarGridSpec(
                num_scalar_prefetch=1,
                grid=(n_groups,),
                in_specs=first_in_specs + [whole(mix), whole(pick)],
                out_specs=part_specs[k * ways : (k + 1) * ways],
                scratch_shapes=[pltpu.VMEM((ways * size * tile, rows), BF16)],
            ),
            out_shape=part_shapes[k * ways : (k + 1) * ways],
            compiler_params=params(),
            cost_estimate=cost(moved * BLOCK_IN * size / here * 5, moved),
            name="lead",
        )(me, tokens, cotangent, right_one, left_two, mix, pick)

    lane_done = {}

    def send(parts, m):
        part = parts[m]
        if m // 2 in lane_done:
            part, _ = lax.optimization_barrier((part, lane_done[m // 2]))
        taken = lax.ppermute(part, "block", [(i, i ^ m) for i in range(ways)])
        lane_done[m // 2] = taken
        return taken

    def send_all(parts, ms):
        return {m: send(parts, m) for m in ms}

    evens = list(range(2, ways, 2))
    odds = list(range(1, ways, 2))
    near = [m for m in range(2, ways) if (m // 2) & (m // 2 - 1) == 0]
    everyone = evens + odds

    share = (BLOCK_HID * MIDDLE + MIDDLE * BLOCK_HID) // n_dp // LANES
    def middle(k, takes, old, first_give, n_give):
        size, at = chunks[k], offsets[k]
        slice_spec = pl.BlockSpec((2, 1, span, rows), lambda i, me: (0, i, 0, 0))
        give_spec = pl.BlockSpec((2, 1, span, rows), lambda i, me: (0, i + first_give, 0, 0))
        flops = 12 * size * MIDDLE * BLOCK_HID * rows
        return pl.pallas_call(
            functools.partial(middle_kernel, ways, len(old), n_dp, scale),
            grid_spec=pltpu.PrefetchScalarGridSpec(
                num_scalar_prefetch=1,
                grid=(size,),
                in_specs=[slice_spec] * ways
                + [
                    pl.BlockSpec((1, MIDDLE, BLOCK_HID), lambda i, me: (i + at, 0, 0)),
                    pl.BlockSpec((1, BLOCK_HID, MIDDLE), lambda i, me: (i + at, 0, 0)),
                ]
                + [pl.BlockSpec(memory_space=pl.ANY)] * len(old),
                out_specs=[give_spec] * ways
                + [pl.BlockSpec((n_dp, 1, share, LANES), lambda i, me: (0, i, 0, 0))],
                scratch_shapes=[pltpu.VMEM((MIDDLE, rows), BF16)] * 4,
            ),
            out_shape=[pltpu.HBM((2, n_give, span, rows), BF16)] * ways
            + [pltpu.HBM((n_dp, size, share, LANES), BF16)],
            input_output_aliases={ways + 3 + i: i for i in range(len(old))},
            compiler_params=params(),
            cost_estimate=cost(flops, size * MIDDLE * (8 * rows + 8 * BLOCK_HID)),
            name="middle",
        )(me, *in_hbm(takes), left_one, right_two, *in_hbm(old))

    def summed(grads):
        return lax.psum_scatter(grads, "dp", scatter_dimension=0, tiled=True)

    queue = [dict(enumerate(lead(0)))]
    got = [{0: queue[0][0]}]
    for m in near + [m for m in everyone if m not in near]:
        got[0][m] = lax.ppermute(queue[0][m], "block", [(i, i ^ m) for i in range(ways)])
        lane_done[m // 2] = got[0][m]
    queue += [dict(enumerate(lead(k))) for k in range(1, n_parts - 1)]
    rest = pl.pallas_call(
        functools.partial(first_kernel, chunks, n_parts - 1, ways),
        grid_spec=pltpu.PrefetchScalarGridSpec(
            num_scalar_prefetch=1,
            grid=(n_groups,),
            in_specs=first_in_specs + [whole(perm)],
            out_specs=part_specs[-ways:],
            scratch_shapes=[pltpu.VMEM((2, GROUP, MIDDLE, rows), BF16)],
        ),
        out_shape=part_shapes[-ways:],
        compiler_params=params(),
        cost_estimate=cost(moved * BLOCK_IN * 5, 2 * moved),
        name="first",
    )(me, tokens, cotangent, right_one, left_two, perm)
    queue.append(dict(enumerate(rest)))

    early_size = offsets[-1]
    back_chunks = (early_size, chunks[-1])
    big_sums, early, held = [], (), {}
    far = [m for m in everyone if m > 1 and m not in near]
    for k in range(n_parts):
        last_part = k + 1 == n_parts
        if last_part:
            parts = dict(enumerate(early))
            ahead = send_all(parts, [m for m in near if m % 2 == 0])
            for m, before in zip([m for m in near if m % 2], far):
                lane_done[m // 2] = got[k][before]
                ahead[m] = send(parts, m)
            outs = middle(k, [got[k][m] for m in range(ways)], (), 0, chunks[-1])
        else:
            parts = queue[k + 1]
            ahead = send_all(parts, [m for m in near if m % 2 == 0])
            outs = middle(k, [got[k][m] for m in range(ways)], early, offsets[k], early_size)
        held, outs = lax.optimization_barrier((ahead, tuple(outs)))
        big_sums.append(summed(outs[ways]))
        parts = lax.optimization_barrier((parts, held))[0]
        if last_part:
            late = dict(enumerate(outs[:ways]))
        else:
            early = outs[:ways]
            if k + 2 == n_parts:
                for m in far:
                    lane_done.pop(m // 2, None)
                    held[m] = send(parts, m)
                    lane_done.pop(m // 2, None)
            got.append({0: parts[0]} | held | send_all(parts, [m for m in everyone if m not in held]))
    early = parts
    late = lax.optimization_barrier((late, tuple(big_sums[:-1])))[0]
    back = [{0: early[0]} | held, {0: late[0]}]
    for m in far + [1]:
        back[0][m] = lax.ppermute(early[m], "block", [(i, i ^ m) for i in range(ways)])
    evens_near = [m for m in near if m % 2 == 0]
    odds_near = [m for m in near if m % 2]
    for m in evens_near:
        back[1][m] = lax.ppermute(late[m], "block", [(i, i ^ m) for i in range(ways)])
    waits = [(m, back[0][far[i % len(far)]]) for i, m in enumerate(odds_near)]
    waits += [(m, back[1][evens_near[i % len(evens_near)]]) for i, m in enumerate(far)]
    for m, done in waits + [(1, back[0][1])]:
        part, _ = lax.optimization_barrier((late[m], done))
        back[1][m] = lax.ppermute(part, "block", [(i, i ^ m) for i in range(ways)])
    returned = [[taken[m] for m in range(ways)] for taken in back]
    back_specs = [
        pl.BlockSpec((2, size, tile, rows), lambda i, me: (0, 0, i, 0))
        for size in back_chunks
        for _ in range(ways)
    ]

    small_share = 2 * MIDDLE * BLOCK_IN // n_dp // LANES
    grad_tokens, small_grads = pl.pallas_call(
        functools.partial(last_kernel, back_chunks, ways, n_dp, scale),
        grid_spec=pltpu.PrefetchScalarGridSpec(
            num_scalar_prefetch=1,
            grid=(n_groups,),
            in_specs=[token_spec, token_spec, right_spec, whole(perm_back)] + back_specs,
            out_specs=[
                token_spec,
                pl.BlockSpec((n_dp, GROUP, small_share, LANES), lambda i, me: (0, i, 0, 0)),
            ],
            scratch_shapes=[pltpu.VMEM((2, GROUP, MIDDLE, rows), BF16)],
        ),
        out_shape=[
            jax.ShapeDtypeStruct(tokens.shape, BF16),
            pltpu.HBM((n_dp, here, small_share, LANES), BF16),
        ],
        compiler_params=params(),
        cost_estimate=cost(moved * BLOCK_IN * 6, 2 * moved),
        name="last",
    )(me, tokens, cotangent, right_one, perm_back, *in_hbm([part for parts in returned for part in parts]))
    small_grads, _ = lax.optimization_barrier((small_grads, big_sums[-1]))
    small_sum = summed(small_grads)

    big_shapes = ((BLOCK_HID // n_dp, MIDDLE), (MIDDLE // n_dp, BLOCK_HID))
    big = ()
    for k, size in enumerate(chunks):
        big = widen(big_sums[k], big_shapes, here, offsets[k], big, 1)
    grad_right_two, grad_left_one = big
    small_shapes = ((MIDDLE // n_dp, BLOCK_IN), (BLOCK_IN // n_dp, MIDDLE))
    grad_left_two, grad_right_one = widen(small_sum, small_shapes, here, 0, (), here)
    return (
        grad_tokens,
        grad_right_one,
        grad_left_one,
        grad_right_two,
        grad_left_two,
        new_moment_one,
        new_moment_two,
        adam_update,
    )


def gelu_tanh(values):
    return jax.nn.gelu(values, approximate=True)


def on_device_plain(
    tokens, cotangent, right_one, left_one, right_two, left_two, grad_prev, moment_one, moment_two
):
    f32 = jnp.float32
    bf16 = jnp.bfloat16
    row_count = tokens.shape[0]
    blocks_here = right_one.shape[0]
    loss_scale = float(lax.axis_size("dp") * row_count) ** (-0.5)
    new_moment_one = 0.9 * moment_one + 0.1 * grad_prev
    new_moment_two = 0.95 * moment_two + 0.05 * grad_prev * grad_prev
    first_hat = new_moment_one / (1.0 - 0.9**10)
    second_hat = new_moment_two / (1.0 - 0.95**10)
    adam_update = first_hat / (jnp.sqrt(second_hat) + 1e-08)
    token_blocks = tokens.reshape(row_count, blocks_here, BLOCK_IN)
    first_mid = jnp.einsum(
        "tbk,bkj->bjt", token_blocks, right_one, preferred_element_type=f32
    ).astype(bf16)
    first_in = lax.all_to_all(
        first_mid.reshape(blocks_here, BLOCKS, SPLIT, row_count),
        "block",
        split_axis=1,
        concat_axis=0,
        tiled=True,
    )
    left_first = left_one.reshape(blocks_here, BLOCKS, SPLIT, BLOCK_HID)
    hidden_pre = jnp.einsum("bcqt,cbqf->cft", first_in, left_first, preferred_element_type=f32)
    hidden = gelu_tanh(hidden_pre).astype(bf16)
    second_mid = jnp.einsum("cft,cfj->cjt", hidden, right_two, preferred_element_type=f32).astype(
        bf16
    )
    second_in = lax.all_to_all(
        second_mid.reshape(blocks_here, BLOCKS, SPLIT, row_count),
        "block",
        split_axis=1,
        concat_axis=0,
        tiled=True,
    )
    left_second = left_two.reshape(blocks_here, BLOCKS, SPLIT, BLOCK_IN)
    grad_blocks = cotangent.reshape(row_count, blocks_here, BLOCK_IN)
    grad_second_out = jnp.einsum(
        "tdk,dcqk->cdqt", grad_blocks, left_second, preferred_element_type=f32
    ).astype(bf16)
    grad_left_two = (
        jnp.einsum("cdqt,tdk->dcqk", second_in, grad_blocks, preferred_element_type=f32)
        * loss_scale
    )
    grad_left_two = grad_left_two.reshape(blocks_here, MIDDLE, BLOCK_IN)
    grad_second = lax.all_to_all(grad_second_out, "block", split_axis=0, concat_axis=1, tiled=True)
    grad_second = grad_second.reshape(blocks_here, MIDDLE, row_count)
    grad_right_two = (
        jnp.einsum("cft,cjt->cfj", hidden, grad_second, preferred_element_type=f32) * loss_scale
    )
    grad_hidden = jnp.einsum("cjt,cfj->cft", grad_second, right_two, preferred_element_type=f32)
    unused_value, back_gelu = jax.vjp(gelu_tanh, hidden_pre)
    grad_pre = back_gelu(grad_hidden)[0].astype(bf16)
    grad_left_one = (
        jnp.einsum("bcqt,cft->cbqf", first_in, grad_pre, preferred_element_type=f32) * loss_scale
    )
    grad_left_one = grad_left_one.reshape(blocks_here, MIDDLE, BLOCK_HID)
    grad_first_out = jnp.einsum(
        "cft,cbqf->bcqt", grad_pre, left_first, preferred_element_type=f32
    ).astype(bf16)
    grad_first = lax.all_to_all(grad_first_out, "block", split_axis=0, concat_axis=1, tiled=True)
    grad_first = grad_first.reshape(blocks_here, MIDDLE, row_count)
    grad_right_one = (
        jnp.einsum("tbk,bjt->bkj", token_blocks, grad_first, preferred_element_type=f32)
        * loss_scale
    )
    grad_inputs = jnp.einsum(
        "bjt,bkj->tbk", grad_first, right_one, preferred_element_type=f32
    ).astype(bf16)
    grad_tokens = grad_inputs.reshape(row_count, blocks_here * BLOCK_IN)
    sum_right_one, sum_left_one, sum_right_two, sum_left_two = (
        lax.psum_scatter(
            grad_right_one.astype(jnp.bfloat16), "dp", scatter_dimension=1, tiled=True
        ).astype(jnp.float32),
        lax.psum_scatter(
            grad_left_one.astype(jnp.bfloat16), "dp", scatter_dimension=1, tiled=True
        ).astype(jnp.float32),
        lax.psum_scatter(
            grad_right_two.astype(jnp.bfloat16), "dp", scatter_dimension=1, tiled=True
        ).astype(jnp.float32),
        lax.psum_scatter(
            grad_left_two.astype(jnp.bfloat16), "dp", scatter_dimension=1, tiled=True
        ).astype(jnp.float32),
    )
    return (
        grad_tokens,
        sum_right_one,
        sum_left_one,
        sum_right_two,
        sum_left_two,
        new_moment_one,
        new_moment_two,
        adam_update,
    )


def solution(mesh):
    in_specs = (
        P("dp", "block"),
        P("dp", "block"),
        P("block", None, None),
        P("block", None, None),
        P("block", None, None),
        P("block", None, None),
        P("block", "dp"),
        P("block", "dp"),
        P("block", "dp"),
    )
    out_specs = (
        P("dp", "block"),
        P("block", "dp", None),
        P("block", "dp", None),
        P("block", "dp", None),
        P("block", "dp", None),
        P("block", "dp"),
        P("block", "dp"),
        P("block", "dp"),
    )
    here = BLOCKS // mesh.shape["block"]
    ways = mesh.shape["block"]
    fits = here % sum(CHUNKS) == 0 and ways >= 8 and here % GROUP == 0 and ways & (ways - 1) == 0
    return jax.shard_map(
        on_device_fast if fits else on_device_plain, mesh=mesh, in_specs=in_specs, out_specs=out_specs, check_vma=False
    )
```
